32 devices in a mesh: dom: 8 (over z, x), space: 4 (over y, core).
Axes of the slice: x: 2, y: 2, z: 4, core: 2. Of those that a mesh axis runs over, the one named last changes fastest.
Arguments:
- states: float32 [16, 3, 512, 128], P('dom', None, 'space'), may hold values from -6 to 6
- weights: int32 [16], P('dom'), may hold values from 0 to 4095, as said below
- offset_draw: int32 [1], replicated, may hold values from 0 to 15
- obs_cells: int32 [128], P('space'), may hold values from 0 to 16383
- obs_values: float32 [128], P('space'), may hold values from -6 to 6
- obs_precision: float32 [128], P('space'), may hold values from 0.25 to 4
Outputs:
- new_states: float32 [16, 3, 512, 128], P('dom', None, 'space')
- log_likelihood: float32 [16], P('dom')
The draws below stay inside these ranges and needn't reach their ends.
Inputs may be any that keep to these rules, and one draw needn't show every extreme that they name: weights are fixed-point values; exactly one particle, among the first 4, has weight 4095, and every other weight is at most 63.
All inputs are finite; a program needn't handle non-finite values.
Results may differ from the reference program's by a relative error of at most 0.00017.
Values sent between devices are 32-bit elements; how exact they have to be, the bound alone decides.
No kernel may reach another device: no remote copies, remote signals or barrier semaphores. Data moves between devices by JAX's collectives and lax.ppermute only.
A program may use at most 64 MiB of HBM per device.

```python
import math
import jax
import jax.numpy as jnp

LAT_DEV = 128
NLON = 128
FIELDS = 3
STEPS = 2
OBS_DEV = 32
PARTICLES = 16
NLAT = 512
OBS = 128


def draw_weights(key, part):
    key_values, key_peak = jax.random.split(key, 2)
    light_most = 4095 // (4 * PARTICLES)
    values = jax.random.randint(key_values, (PARTICLES,), 0, light_most + 1)
    chosen = jax.random.randint(key_peak, (), 0, PARTICLES // 4)
    return jnp.where(jnp.arange(PARTICLES) == chosen, 4095, values).astype(jnp.int32)


def place_ends(drawn, own_key, least, high):
    spot = [jax.random.randint(jax.random.fold_in(own_key, axis), (), 0, length) for axis, length in enumerate(drawn.shape)]
    widest = drawn.shape.index(max(drawn.shape))
    neighbour = spot[:widest] + [(spot[widest] + 1) % drawn.shape[widest]] + spot[widest + 1:]
    return drawn.at[tuple(spot)].set(least).at[tuple(neighbour)].set(high)


def shard_levels(key, dims, cuts, smallest, top_value):
    factor_of = 1.0
    for dim, shards_of in cuts:
        heights = jax.random.uniform(jax.random.fold_in(jax.random.fold_in(key, 6), dim), (shards_of,), jnp.float32, smallest / len(cuts), top_value / len(cuts))
        factor_of = factor_of * jnp.repeat(jnp.exp(heights), dims[dim] // shards_of).reshape((-1,) + (1,) * (len(dims) - 1 - dim))
    return factor_of


def bell_draw(key, shape, deviation, most, shards=(), kind=jnp.bfloat16):
    entries = deviation * jax.random.normal(key, shape, jnp.float32)
    if shards:
        entries = entries * shard_levels(key, shape, shards, -0.22, 0.18)
    return jnp.clip(entries, -most, most).astype(kind)


def setup_inputs(seed: int = 0) -> dict:
    streams_of = jax.random.split(jax.random.key(seed), 7)
    states = bell_draw(streams_of[0], (PARTICLES, FIELDS, NLAT, NLON), 1.0, 6.0, ((0, 8), (2, 4)), jnp.float32)
    weights = draw_weights(jax.random.fold_in(streams_of[6], 71), 0)
    offset_draw = jax.random.randint(streams_of[2], (1,), 0, PARTICLES).astype(jnp.int32)
    obs_cells = place_ends(jax.random.randint(streams_of[3], (OBS,), 0, LAT_DEV * NLON), jax.random.fold_in(streams_of[3], 1), 0, (LAT_DEV * NLON) - 1).astype(jnp.int32)
    obs_values = bell_draw(streams_of[4], (OBS,), 1.0, 6.0, ((0, 4),), jnp.float32)
    obs_precision = jnp.clip(jnp.exp(math.log(4.0) - 2.7725887 * jax.random.uniform(streams_of[5], (OBS,), jnp.float32) ** shard_levels(streams_of[5], (OBS,), ((0, 4),), -0.2, 0.2)), 0.25, 4.0)
    return {"states": states, "weights": weights, "offset_draw": offset_draw, "obs_cells": obs_cells, "obs_values": obs_values, "obs_precision": obs_precision}


ADVECT = 0.25
DIFFUSE = 0.2


def advance(padded):
    center = padded[:, :, 1:-1]
    upper_row = padded[:, :, 2:]
    lower_row = padded[:, :, :-2]
    east_cell = jnp.roll(center, -1, axis=3)
    west_cell = jnp.roll(center, 1, axis=3)
    zonal_flow = center[:, 0:1]
    merid_flow = center[:, 1:2]
    transport = zonal_flow * (east_cell - west_cell) + merid_flow * (upper_row - lower_row)
    spread = east_cell + west_cell + upper_row + lower_row - 4.0 * center
    return center - (0.5 * ADVECT) * transport + DIFFUSE * spread


def slot_bounds(before, weight_sum, offset, particles):
    numerator = particles * before - (offset * weight_sum) // particles
    ceiling = -((-numerator) // weight_sum)
    return jnp.clip(ceiling, 0, particles).astype(jnp.int32)


def reference(states, weights, offset_draw, obs_cells, obs_values, obs_precision):
    before = (jnp.cumsum(weights) - weights).astype(jnp.int32)
    weight_sum = jnp.sum(weights).astype(jnp.int32)
    starts = slot_bounds(before, weight_sum, offset_draw[0], PARTICLES)
    slot_ids = jnp.arange(PARTICLES, dtype=jnp.int32)
    ancestors = (jnp.sum((starts[None, :] <= slot_ids[:, None]).astype(jnp.int32), axis=1) - 1).astype(jnp.int32)
    offspring = jnp.take(states, ancestors, axis=0)
    for iteration in range(STEPS):
        padded = jnp.pad(offspring, ((0, 0), (0, 0), (1, 1), (0, 0)))
        offspring = advance(padded)
    height = offspring[:, 2].reshape(PARTICLES, NLAT * NLON)
    slab_base = (jnp.arange(OBS, dtype=jnp.int32) // OBS_DEV) * (LAT_DEV * NLON)
    where_obs = (slab_base + obs_cells).astype(jnp.int32)
    observed = jnp.take(height, where_obs, axis=1)
    misfit = jnp.sum(obs_precision[None, :] * (observed - obs_values[None, :]) ** 2, axis=1)
    return offspring, -0.5 * misfit / OBS
```

```python
import jax
import jax.numpy as jnp
from jax import lax
from jax.experimental import pallas as pl
from jax.experimental.pallas import tpu as pltpu
from jax.sharding import PartitionSpec as P

STEPS = 2
ADVECT = 0.25
DIFFUSE = 0.2
HEAVY = 4095
PAD = 8


LIMIT = pltpu.CompilerParams(vmem_limit_bytes=6 * 1024 * 1024)
SMEM = pl.BlockSpec(memory_space=pltpu.SMEM)
VMEM = pl.BlockSpec(memory_space=pltpu.VMEM)
ANY = pl.BlockSpec(memory_space=pl.ANY)


def move_kernel(w_ref, cells_ref, values_ref, precision_ref, states_ref, above_ref, below_ref,
                moved_ref, heavy_ref, misfit_ref, work_a, work_b):
    count, fields, rows, lons = states_ref.shape
    obs = cells_ref.shape[0]
    slab, slabs = lax.axis_index("space"), lax.axis_size("space")
    inner = pl.ds(PAD, rows)
    keep_low = (slab > 0).astype(jnp.float32)
    keep_high = (slab < slabs - 1).astype(jnp.float32)
    lanes = lax.broadcasted_iota(jnp.int32, (1, lons), 1)
    work = (work_a, work_b)

    def stepped(src, first, length):
        center = [src[f, pl.ds(first, length), :] for f in range(fields)]
        out = []
        for f in range(fields):
            upper = src[f, pl.ds(first + 1, length), :]
            lower = src[f, pl.ds(first - 1, length), :]
            east = pltpu.roll(center[f], lons - 1, 1)
            west = pltpu.roll(center[f], 1, 1)
            transport = center[0] * (east - west) + center[1] * (upper - lower)
            spread = east + west + upper + lower - 4.0 * center[f]
            out.append(center[f] - 0.5 * ADVECT * transport + DIFFUSE * spread)
        return out

    for p in range(count):
        work_a[:, inner, :] = states_ref[p]
        work_a[:, pl.ds(PAD - STEPS, STEPS), :] = below_ref[p]
        work_a[:, pl.ds(PAD + rows, STEPS), :] = above_ref[p]
        block = 16
        for step in range(STEPS):
            src = work[step % 2]
            last = step == STEPS - 1
            margin = STEPS - 1 - step
            if not last:
                dst = work[(step + 1) % 2]
                low = stepped(src, PAD - margin, margin)
                high = stepped(src, PAD + rows, margin)
                for f in range(fields):
                    dst[f, pl.ds(PAD - margin, margin), :] = low[f] * keep_low
                    dst[f, pl.ds(PAD + rows, margin), :] = high[f] * keep_high
            for b in range(0, rows, block):
                new = stepped(src, PAD + b, block)
                for f in range(fields):
                    if last:
                        moved_ref[p, f, pl.ds(b, block), :] = new[f]
                    else:
                        dst[f, pl.ds(PAD + b, block), :] = new[f]
        total = [jnp.zeros((1, lons), jnp.float32)] * 4
        for o in range(obs):
            cell = cells_ref[o]
            row = moved_ref[p, fields - 1, pl.ds(cell // lons, 1), :]
            gap = row - values_ref[o]
            total[o % 4] = total[o % 4] + jnp.where(lanes == cell % lons, precision_ref[o] * (gap * gap), 0.0)
        misfit_ref[pl.ds(p, 1), :] = (total[0] + total[1]) + (total[2] + total[3])

    place = jnp.int32(count)
    for p in range(count):
        place = jnp.where(w_ref[p] == HEAVY, p, place)

    @pl.when(place < count)
    def _():
        heavy_ref[...] = moved_ref[place]

    @pl.when(place == count)
    def _():
        heavy_ref[...] = jnp.zeros(heavy_ref.shape, jnp.float32)


def move(states, above, below, weights, obs_cells, obs_values, obs_precision):
    count, fields, rows, lons = states.shape
    return pl.pallas_call(
        move_kernel,
        out_shape=(
            jax.ShapeDtypeStruct(states.shape, jnp.float32),
            jax.ShapeDtypeStruct(states.shape[1:], jnp.float32),
            jax.ShapeDtypeStruct((count, lons), jnp.float32),
        ),
        in_specs=[SMEM] * 4 + [VMEM] * 3,
        out_specs=(VMEM, VMEM, VMEM),
        scratch_shapes=[pltpu.VMEM((fields, rows + 2 * PAD, lons), jnp.float32)] * 2,
        cost_estimate=pl.CostEstimate(flops=40 * states.size, bytes_accessed=12 * states.size, transcendentals=0),
        compiler_params=LIMIT,
    )(weights, obs_cells, obs_values, obs_precision, states, above, below)


def plan_kernel(slots, offset_ref, w_ref, ancestor_ref, code_ref):
    total, lanes = w_ref.shape
    w = w_ref[...]
    row = lax.broadcasted_iota(jnp.int32, (total, lanes), 0)
    lane = lax.broadcasted_iota(jnp.int32, (total, lanes), 1)
    before = jnp.sum(jnp.where(row < lane, w, 0), axis=0, keepdims=True)
    weight_sum = jnp.sum(w, axis=0, keepdims=True)
    heavy = jnp.sum(jnp.where(w == HEAVY, row, 0), axis=0, keepdims=True)
    shift = (offset_ref[0] * weight_sum) // total
    reached = (total * before - shift <= row * weight_sum) & (lane < total)
    ancestor = jnp.sum(reached.astype(jnp.int32), axis=1, keepdims=True) - 1
    ancestor = jnp.broadcast_to(ancestor, (total, lanes))
    ancestor_ref[...] = ancestor
    width = total.bit_length()
    entry = ancestor + jnp.where(ancestor == heavy, 0, 1 << (width - 1))
    code = jnp.zeros((1, lanes), jnp.int32)
    for n, slot in enumerate(slots):
        code = code + entry[slot:slot + 1] * (1 << (n * width))
    code_ref[0] = code[0, 0]


def plan(every_weight, offset, slots):
    return pl.pallas_call(
        lambda *refs: plan_kernel(slots, *refs),
        out_shape=(jax.ShapeDtypeStruct(every_weight.shape, jnp.int32), jax.ShapeDtypeStruct((1,), jnp.int32)),
        in_specs=[SMEM, VMEM],
        out_specs=(VMEM, SMEM),
        compiler_params=LIMIT,
    )(offset, every_weight)


def finish_kernel(slots, observations, code_ref, ancestor_ref, misfit_ref, heavy_ref, *rest):
    lights, (out_ref, likelihood_ref, sems) = rest[:len(slots)], rest[len(slots):]
    count, total = out_ref.shape[0], ancestor_ref.shape[0]
    width = total.bit_length()
    here = lax.axis_index("dom")
    for k in range(count):
        taken = jnp.bool_(False)
        for n, slot in enumerate(slots):
            if slot % count == k:
                light = (here == slot // count) & (((code_ref[0] >> (n * width + width - 1)) & 1) == 1)
                taken = taken | light

                @pl.when(light)
                def _():
                    pltpu.make_async_copy(lights[n], out_ref.at[k], sems.at[k]).start()

        @pl.when(jnp.logical_not(taken))
        def _():
            pltpu.make_async_copy(heavy_ref, out_ref.at[k], sems.at[k]).start()

    row = lax.broadcasted_iota(jnp.int32, misfit_ref.shape, 0)
    for k in range(count):
        parent = ancestor_ref[pl.ds(here * count + k, 1), :]
        likelihood_ref[k] = -0.5 * jnp.sum(jnp.where(row == parent, misfit_ref[...], 0.0)) / observations
    for k in range(count):
        pltpu.make_async_copy(heavy_ref, out_ref.at[k], sems.at[k]).wait()


def finish(count, slots, observations, code, ancestor, misfit, heavy, lights):
    return pl.pallas_call(
        lambda *refs: finish_kernel(slots, observations, *refs),
        out_shape=(
            jax.ShapeDtypeStruct((count,) + heavy.shape, jnp.float32),
            jax.ShapeDtypeStruct((count,), jnp.float32),
        ),
        in_specs=[SMEM, VMEM, VMEM, ANY] + [ANY] * len(lights),
        out_specs=(ANY, SMEM),
        scratch_shapes=[pltpu.SemaphoreType.DMA((count,))],
        compiler_params=LIMIT,
    )(code, ancestor, misfit, heavy, *lights)


def gathered(part, axis):
    size, place = lax.axis_size(axis), lax.axis_index(axis)
    bit = 1
    while bit < size:
        other = lax.ppermute(part, axis, [(i, i ^ bit) for i in range(size)])
        part = jnp.where((place & bit) == 0, jnp.concatenate([part, other]), jnp.concatenate([other, part]))
        bit *= 2
    return part


def summed(part, axis):
    size = lax.axis_size(axis)
    bit = 1
    while bit < size:
        part = part + lax.ppermute(part, axis, [(i, i ^ bit) for i in range(size)])
        bit *= 2
    return part


def spread_heavy(heavy, owners, size):
    bit = 1
    while bit < owners:
        heavy = heavy + lax.ppermute(heavy, "dom", [(i, i ^ bit) for i in range(owners)])
        bit *= 2
    bit = size // 2
    while bit >= owners:
        pairs = [(i, i + bit) for i in range(0, size) if (i // owners) % (2 * bit // owners) == 0]
        heavy = heavy + lax.ppermute(heavy, "dom", pairs)
        bit //= 2
    return heavy


def light_slots(total):
    most = HEAVY // (4 * total)
    head = (total // 4 - 1) * most
    tail = (total - 1) * most
    first = -(-total * head // (HEAVY + head))
    last = (total * tail * total + (total - 1) * (HEAVY + tail)) // (total * (HEAVY + tail))
    return list(range(first)) + list(range(total - last, total))


def local(states, weights, offset_draw, obs_cells, obs_values, obs_precision):
    count, fields, rows, lons = states.shape
    size = lax.axis_size("dom")
    slabs = lax.axis_size("space")
    total = count * size
    observations = obs_cells.shape[0] * slabs
    below = lax.ppermute(states[:, :, rows - STEPS:], "space", [(i, i + 1) for i in range(slabs - 1)])
    above = lax.ppermute(states[:, :, :STEPS], "space", [(i + 1, i) for i in range(slabs - 1)])
    every_weight = gathered(jnp.broadcast_to(weights[:, None], (count, max(lons, total))), "dom")
    moved, heavy, misfit = move(states, above, below, weights, obs_cells, obs_values, obs_precision)
    every_misfit = gathered(summed(misfit, "space"), "dom")
    if size > 8:
        ancestor, _ = plan(every_weight, offset_draw, [])
        mine = lax.dynamic_slice_in_dim(ancestor[:, 0], lax.axis_index("dom") * count, count)
        everything = lax.all_gather(moved, "dom", axis=0, tiled=True)
        likelihood = -0.5 * jnp.sum(jnp.take(every_misfit, mine, axis=0), axis=1) / observations
        return jnp.take(everything, mine, axis=0), likelihood
    slots = light_slots(total)
    ancestor, code = plan(every_weight, offset_draw, slots)
    owners = max(1, total // 4 // count)
    heavy = spread_heavy(heavy, owners, size)
    width = total.bit_length()
    lights = []
    for n, slot in enumerate(slots):
        target = slot // count

        def branch(device):
            def run(moved, place):
                piece = lax.dynamic_index_in_dim(moved, place, 0, keepdims=False)
                if device == target:
                    return piece
                return lax.ppermute(piece, "dom", [(device, target)])
            return run

        entry = (code[0] >> (n * width)) & (2 * total - 1)
        reach = size if slot >= count else owners
        index = jnp.where(entry >= total, (entry - total) // count, reach)
        none = lambda moved, place: jnp.zeros(moved.shape[1:], moved.dtype)
        lights.append(lax.switch(index, [branch(d) for d in range(reach)] + [none], moved, entry % count))
    return finish(count, slots, observations, code, ancestor, every_misfit, heavy, lights)


def solution(mesh):
    return jax.shard_map(
        local,
        mesh=mesh,
        in_specs=(P("dom", None, "space", None), P("dom"), P(), P("space"), P("space"), P("space")),
        out_specs=(P("dom", None, "space", None), P("dom")),
        check_vma=False,
    )
```

```python
import jax
import jax.numpy as jnp
from jax import lax
from jax.experimental import pallas as pl
from jax.experimental.pallas import tpu as pltpu
from jax.sharding import PartitionSpec as P

STEPS = 2
ADVECT = 0.25
DIFFUSE = 0.2
HEAVY = 4095
PAD = 8
EXTRA = 8

LIMIT = pltpu.CompilerParams(vmem_limit_bytes=6 * 1024 * 1024)
SMEM = pl.BlockSpec(memory_space=pltpu.SMEM)
VMEM = pl.BlockSpec(memory_space=pltpu.VMEM)
ANY = pl.BlockSpec(memory_space=pl.ANY)


def shape_of(shape, dtype=jnp.float32):
    return jax.ShapeDtypeStruct(shape, dtype)


def open_kernel(w_ref, states_ref, near_ref, far_ref, rows_ref, copy_ref):
    count, fields, rows, lons = states_ref.shape
    even = lax.axis_index("space") % 2 == 0
    top = states_ref[:, :, pl.ds(0, STEPS), :]
    bottom = states_ref[:, :, pl.ds(rows - STEPS, STEPS), :]
    near_ref[...] = jnp.where(even, bottom, top)
    far_ref[...] = jnp.where(even, top, bottom)
    for p in range(count):
        rows_ref[pl.ds(p, 1), :] = jnp.full((1, rows_ref.shape[1]), w_ref[p], jnp.int32)
    copy_ref[...] = states_ref[...]


def opening(states, weights, lanes):
    count, fields, rows, lons = states.shape
    edge = (count, fields, STEPS, lons)
    return pl.pallas_call(
        open_kernel,
        out_shape=(shape_of(edge), shape_of(edge), shape_of((count, lanes), jnp.int32), shape_of(states.shape)),
        in_specs=[SMEM, VMEM],
        out_specs=(VMEM, VMEM, VMEM, VMEM),
        compiler_params=LIMIT,
    )(weights, states)


def move_kernel(w_ref, cells_ref, values_ref, precision_ref, states_ref, near_ref, far_ref,
                moved_ref, heavy_ref, work_a, work_b):
    count, fields, rows, lons = states_ref.shape
    obs = cells_ref.shape[0]
    slab, slabs = lax.axis_index("space"), lax.axis_size("space")
    even = slab % 2 == 0
    inner = pl.ds(PAD, rows)
    has_low, has_high = slab > 0, slab < slabs - 1
    lanes = lax.broadcasted_iota(jnp.int32, (1, lons), 1)
    work = (work_a, work_b)

    def stepped(src, first, length):
        center = [src[f, pl.ds(first, length), :] for f in range(fields)]
        out = []
        for f in range(fields):
            upper = src[f, pl.ds(first + 1, length), :]
            lower = src[f, pl.ds(first - 1, length), :]
            east = pltpu.roll(center[f], lons - 1, 1)
            west = pltpu.roll(center[f], 1, 1)
            transport = center[0] * (east - west) + center[1] * (upper - lower)
            spread = east + west + upper + lower - 4.0 * center[f]
            out.append(center[f] - 0.5 * ADVECT * transport + DIFFUSE * spread)
        return out

    for p in range(count):
        near, far = near_ref[p], far_ref[p]
        work_a[:, inner, :] = states_ref[p]
        work_a[:, pl.ds(PAD - STEPS, STEPS), :] = jnp.where(has_low, jnp.where(even, far, near), 0.0)
        work_a[:, pl.ds(PAD + rows, STEPS), :] = jnp.where(has_high, jnp.where(even, near, far), 0.0)
        block = 16
        for step in range(STEPS):
            src = work[step % 2]
            last = step == STEPS - 1
            margin = STEPS - 1 - step
            if not last:
                dst = work[(step + 1) % 2]
                low = stepped(src, PAD - margin, margin)
                high = stepped(src, PAD + rows, margin)
                for f in range(fields):
                    dst[f, pl.ds(PAD - margin, margin), :] = jnp.where(has_low, low[f], 0.0)
                    dst[f, pl.ds(PAD + rows, margin), :] = jnp.where(has_high, high[f], 0.0)
            for b in range(0, rows, block):
                new = stepped(src, PAD + b, block)
                for f in range(fields):
                    if last:
                        moved_ref[p, pl.ds(f * rows + b, block), :] = new[f]
                    else:
                        dst[f, pl.ds(PAD + b, block), :] = new[f]
        total = [jnp.zeros((1, lons), jnp.float32)] * 4
        for o in range(obs):
            cell = cells_ref[o]
            row = moved_ref[p, pl.ds((fields - 1) * rows + cell // lons, 1), :]
            gap = row - values_ref[o]
            total[o % 4] = total[o % 4] + jnp.where(lanes == cell % lons, precision_ref[o] * (gap * gap), 0.0)
        moved_ref[p, pl.ds(fields * rows, 1), :] = (total[0] + total[1]) + (total[2] + total[3])
        moved_ref[p, pl.ds(fields * rows + 1, EXTRA - 1), :] = jnp.zeros((EXTRA - 1, lons), jnp.float32)

    place = jnp.int32(count)
    for p in range(count):
        place = jnp.where(w_ref[p] == HEAVY, p, place)

    @pl.when(place < count)
    def _():
        heavy_ref[...] = moved_ref[place]

    @pl.when(place == count)
    def _():
        heavy_ref[...] = jnp.zeros(heavy_ref.shape, jnp.float32)


def move(states, near, far, weights, obs_cells, obs_values, obs_precision):
    count, fields, rows, lons = states.shape
    tall = fields * rows + EXTRA
    return pl.pallas_call(
        move_kernel,
        out_shape=(shape_of((count, tall, lons)), shape_of((tall, lons))),
        in_specs=[SMEM] * 4 + [VMEM] * 3,
        out_specs=(VMEM, VMEM),
        scratch_shapes=[pltpu.VMEM((fields, rows + 2 * PAD, lons), jnp.float32)] * 2,
        cost_estimate=pl.CostEstimate(flops=40 * states.size, bytes_accessed=12 * states.size, transcendentals=0),
        compiler_params=LIMIT,
    )(weights, obs_cells, obs_values, obs_precision, states, near, far)


def entries_of(offset, w, heavy_weight=HEAVY):
    total, lanes = w.shape
    row = lax.broadcasted_iota(jnp.int32, (total, lanes), 0)
    lane = lax.broadcasted_iota(jnp.int32, (total, lanes), 1)
    before = jnp.sum(jnp.where(row < lane, w, 0), axis=0, keepdims=True)
    weight_sum = jnp.sum(w, axis=0, keepdims=True)
    heavy = jnp.sum(jnp.where(w == heavy_weight, row, 0), axis=0, keepdims=True)
    shift = (offset * weight_sum) // total
    reached = (total * before - shift <= row * weight_sum) & (lane < total)
    ancestor = jnp.sum(reached.astype(jnp.int32), axis=1, keepdims=True) - 1
    ancestor = jnp.broadcast_to(ancestor, (total, lanes))
    return ancestor + jnp.where(ancestor == heavy, 0, total)


def general_kernel(offset_ref, w_ref, out_ref):
    out_ref[...] = entries_of(offset_ref[0], w_ref[...])


def plan_kernel(slots, offset_ref, w_ref, moved_ref, kind_ref, entry_ref, *piece_refs):
    total, count = w_ref.shape[0], moved_ref.shape[0]
    size = total // count
    entry = entries_of(offset_ref[0], w_ref[...])
    found = {slot: entry[slot, 0] for slot in slots}
    for n, slot in enumerate(slots):
        entry_ref[n] = found[slot]
    last = found[total - 1]
    kind = jnp.where(last >= total, 1 + (last - total) // count, 0)
    for slot in slots:
        if slot < total - len(piece_refs):
            kind = jnp.where(found[slot] >= total, 1 + size, kind)
    kind_ref[0] = kind
    for n, piece_ref in enumerate(piece_refs):
        piece_ref[...] = moved_ref[found[total - 1 - n] % count]


def plan(every_weight, offset, moved, slots, pieces):
    return pl.pallas_call(
        lambda *refs: plan_kernel(slots, *refs),
        out_shape=(shape_of((1,), jnp.int32), shape_of((len(slots),), jnp.int32))
        + (shape_of(moved.shape[1:]),) * pieces,
        in_specs=[SMEM, VMEM, VMEM],
        out_specs=(SMEM, SMEM) + (VMEM,) * pieces,
        compiler_params=LIMIT,
    )(offset, every_weight, moved)


def finish_kernel(slots, flag_ref, heavy_ref, *rest):
    lights, (out_ref, part_ref, sems) = rest[:len(slots)], rest[len(slots):]
    count, tall, lons = out_ref.shape
    here = lax.axis_index("dom")

    def put(ref, k):
        return pltpu.make_async_copy(ref.at[pl.ds(0, tall), :], out_ref.at[k], sems.at[k])

    for k in range(count):
        taken = jnp.bool_(False)
        for n, slot in enumerate(slots):
            if slot % count == k:
                light = (here == slot // count) & (flag_ref[n] > 0)
                taken = taken | light

                @pl.when(light)
                def _():
                    put(lights[n], k).start()
                    part_ref[pl.ds(k, 1), :] = lights[n][pl.ds(tall, 1), :]

        @pl.when(jnp.logical_not(taken))
        def _():
            put(heavy_ref, k).start()
            part_ref[pl.ds(k, 1), :] = heavy_ref[pl.ds(tall, 1), :]

    for k in range(count):
        put(heavy_ref, k).wait()


def finish(count, slots, flags, heavy, lights):
    tall, lons = heavy.shape
    return pl.pallas_call(
        lambda *refs: finish_kernel(slots, *refs),
        out_shape=(shape_of((count, tall - EXTRA, lons)), shape_of((count, lons))),
        in_specs=[SMEM, VMEM] + [VMEM] * len(lights),
        out_specs=(ANY, VMEM),
        scratch_shapes=[pltpu.SemaphoreType.DMA((count,))],
        compiler_params=LIMIT,
    )(flags, heavy, *lights)


def gathered(part, axis):
    size, place = lax.axis_size(axis), lax.axis_index(axis)
    bit = 1
    while bit < size:
        other = lax.ppermute(part, axis, [(i, i ^ bit) for i in range(size)])
        part = jnp.where((place & bit) == 0, jnp.concatenate([part, other]), jnp.concatenate([other, part]))
        bit *= 2
    return part


def summed(part, axis):
    size = lax.axis_size(axis)
    bit = 1
    while bit < size:
        part = part + lax.ppermute(part, axis, [(i, i ^ bit) for i in range(size)])
        bit *= 2
    return part


def shared_heavy(heavy, owners, size):
    bit = 1
    while bit < owners:
        heavy = heavy + lax.ppermute(heavy, "dom", [(i, i ^ bit) for i in range(owners)])
        bit *= 2
    return heavy


def heavy_step(heavy, owners, size, bit):
    pairs = [(i, i + bit) for i in range(0, size) if (i // owners) % (2 * bit // owners) == 0]
    return heavy + lax.ppermute(heavy, "dom", pairs)


def light_slots(total):
    most = HEAVY // (4 * total)
    head = (total // 4 - 1) * most
    tail = (total - 1) * most
    first = -(-total * head // (HEAVY + head))
    last = (total * tail * total + (total - 1) * (HEAVY + tail)) // (total * (HEAVY + tail))
    return list(range(first)) + list(range(total - last, total))


def local(states, weights, offset_draw, obs_cells, obs_values, obs_precision):
    count, fields, rows, lons = states.shape
    size = lax.axis_size("dom")
    slabs = lax.axis_size("space")
    total = count * size
    observations = obs_cells.shape[0] * slabs
    near, far, weight_rows, states = opening(states, weights, max(lons, total))
    near = lax.ppermute(near, "space", [(i, i ^ 1) for i in range(slabs)])
    far = lax.ppermute(far, "space", [(i, (i + 1 if i % 2 else i - 1) % slabs) for i in range(slabs)])
    every_weight = gathered(weight_rows, "dom")
    moved, heavy = move(states, near, far, weights, obs_cells, obs_values, obs_precision)
    if size > 8:
        entry = pl.pallas_call(
            general_kernel, out_shape=shape_of(every_weight.shape, jnp.int32), in_specs=[SMEM, VMEM], out_specs=VMEM,
        )(offset_draw, every_weight)
        mine = lax.dynamic_slice_in_dim(entry[:, 0] % total, lax.axis_index("dom") * count, count)
        everything = lax.all_gather(moved, "dom", axis=0, tiled=True)
        taken = jnp.take(everything, mine, axis=0)
        misfit = lax.psum(jnp.sum(taken[:, fields * rows], axis=1), "space")
        return taken[:, :fields * rows].reshape(states.shape), -0.5 * misfit / observations
    slots = light_slots(total)
    owners = max(1, total // 4 // count)
    kind, entries, piece, second_piece = plan(every_weight, offset_draw, moved, slots, 2)
    heavy = shared_heavy(heavy, owners, size)
    bit = size // 2
    while bit > owners:
        heavy = heavy_step(heavy, owners, size, bit)
        bit //= 2
    last, second = total - 1, total - 2

    def send(part, slot, device):
        target = slot // count
        return part if device == target else lax.ppermute(part, "dom", [(device, target)])

    def maybe(part, slot, n, reach):
        ways = [lambda device=device: send(part, slot, device) for device in range(reach)]
        ways.append(lambda: jnp.zeros(part.shape, part.dtype))
        return lax.switch(jnp.where(entries[n] >= total, (entries[n] - total) // count, reach), ways)

    def none():
        return finish(count, [], jnp.ones((1,), jnp.int32), heavy_step(heavy, owners, size, bit), [])

    def known(device):
        def run():
            n = slots.index(second)
            flags = jnp.stack([jnp.int32(1), (entries[n] >= total).astype(jnp.int32)])
            lights = [send(piece, last, device), maybe(second_piece, second, n, device + 1)]
            return finish(count, [last, second], flags, heavy_step(heavy, owners, size, bit), lights)
        return run

    def mixed():
        lights = []
        for n, slot in enumerate(slots):
            part = lax.dynamic_index_in_dim(moved, entries[n] % count, 0, keepdims=False)
            lights.append(maybe(part, slot, n, size if slot >= count else owners))
        flags = (entries >= total).astype(jnp.int32)
        return finish(count, slots, flags, heavy_step(heavy, owners, size, bit), lights)

    out, part = lax.switch(kind[0], [none] + [known(d) for d in range(size)] + [mixed])
    misfit = jnp.sum(summed(part, "space"), axis=1)
    return out.reshape(states.shape), -0.5 * misfit / observations


def solution(mesh):
    return jax.shard_map(
        local,
        mesh=mesh,
        in_specs=(P("dom", None, "space", None), P("dom"), P(), P("space"), P("space"), P("space")),
        out_specs=(P("dom", None, "space", None), P("dom")),
        check_vma=False,
    )
```

```python
import jax
import jax.numpy as jnp
from jax import lax
from jax.experimental import pallas as pl
from jax.experimental.pallas import tpu as pltpu
from jax.sharding import PartitionSpec as P

STEPS = 2
ADVECT = 0.25
DIFFUSE = 0.2
HEAVY = 4095
PAD = 8
FIELD = 8
TILE = 8

LIMIT = pltpu.CompilerParams(vmem_limit_bytes=6 * 1024 * 1024)
SMEM = pl.BlockSpec(memory_space=pltpu.SMEM)
VMEM = pl.BlockSpec(memory_space=pltpu.VMEM)


def shape_of(shape, dtype=jnp.float32):
    return jax.ShapeDtypeStruct(shape, dtype)


def halo_rows(fields):
    return -(-2 * STEPS * fields // TILE) * TILE


def open_kernel(w_ref, states_ref, near_ref, far_ref, copy_ref, heavy_ref):
    count, fields, rows, lons = states_ref.shape
    even = lax.axis_index("space") % 2 == 0
    top = states_ref[:, :, pl.ds(0, STEPS), :]
    bottom = states_ref[:, :, pl.ds(rows - STEPS, STEPS), :]
    near_ref[...] = jnp.where(even, bottom, top)
    far_ref[...] = jnp.where(even, top, bottom)
    for f in range(fields):
        for b in range(0, rows, 32):
            block = pl.ds(b, 32)
            whole = jnp.zeros((32, lons), jnp.float32)
            for p in range(count):
                part = states_ref[p, f, block, :]
                copy_ref[p, f, block, :] = part
                whole = jnp.where(w_ref[pl.ds(p, 1), :lons] == HEAVY, part, whole)
            heavy_ref[pl.ds(f * rows + b, 32), :] = whole


def opening(weight_rows, states):
    count, fields, rows, lons = states.shape
    edge = (count, fields, STEPS, lons)
    return pl.pallas_call(
        open_kernel,
        out_shape=(shape_of(edge), shape_of(edge), shape_of(states.shape), shape_of((fields * rows, lons))),
        in_specs=[VMEM, VMEM],
        out_specs=(VMEM,) * 4,
        compiler_params=LIMIT,
    )(weight_rows, states)


def pad_kernel(w_ref, states_ref, near_ref, far_ref, padded_ref, halo_ref):
    count, fields, rows, lons = states_ref.shape
    slab, slabs = lax.axis_index("space"), lax.axis_size("space")
    even = slab % 2 == 0
    extra = halo_ref.shape[0]
    halo_ref[...] = jnp.zeros(halo_ref.shape, jnp.float32)
    for p in range(count):
        for f in range(fields):
            padded_ref[p, pl.ds(f * rows, rows), :] = states_ref[p, f]
        padded_ref[p, pl.ds(fields * rows, extra), :] = jnp.zeros((extra, lons), jnp.float32)
        for f in range(fields):
            near, far = near_ref[p, f], far_ref[p, f]
            below = jnp.where(slab > 0, jnp.where(even, far, near), 0.0)
            above = jnp.where(slab < slabs - 1, jnp.where(even, near, far), 0.0)
            at = fields * rows + 2 * STEPS * f
            padded_ref[p, pl.ds(at, STEPS), :] = below
            padded_ref[p, pl.ds(at + STEPS, STEPS), :] = above
        halo = padded_ref[p, pl.ds(fields * rows, extra), :]
        halo_ref[...] = jnp.where(w_ref[pl.ds(p, 1), :lons] == HEAVY, halo, halo_ref[...])


def padding(weight_rows, states, near, far):
    count, fields, rows, lons = states.shape
    extra = halo_rows(fields)
    return pl.pallas_call(
        pad_kernel,
        out_shape=(shape_of((count, fields * rows + extra, lons)), shape_of((extra, lons))),
        in_specs=[VMEM] * 4,
        out_specs=(VMEM, VMEM),
        compiler_params=LIMIT,
    )(weight_rows, states, near, far)


def join_kernel(obs_ref, core_ref, other_core_ref, halo_ref, other_halo_ref, out_ref, obs_copy_ref):
    obs_copy_ref[...] = obs_ref[...]
    tall, extra = core_ref.shape[0], halo_ref.shape[0]
    out_ref[pl.ds(0, tall), :] = core_ref[...] + other_core_ref[...]
    out_ref[pl.ds(tall, extra), :] = halo_ref[...] + other_halo_ref[...]


def joined(obs, core, other_core, halo, other_halo):
    return pl.pallas_call(
        join_kernel,
        out_shape=(shape_of((core.shape[0] + halo.shape[0], core.shape[1])), shape_of(obs.shape)),
        in_specs=[VMEM] * 5,
        out_specs=(VMEM, VMEM),
        compiler_params=LIMIT,
    )(obs, core, other_core, halo, other_halo)


def entries_of(offset, w):
    total, lanes = w.shape
    row = lax.broadcasted_iota(jnp.int32, (total, lanes), 0)
    lane = lax.broadcasted_iota(jnp.int32, (total, lanes), 1)
    before = jnp.sum(jnp.where(row < lane, w, 0), axis=0, keepdims=True)
    weight_sum = jnp.sum(w, axis=0, keepdims=True)
    heavy = jnp.sum(jnp.where(w == HEAVY, row, 0), axis=0, keepdims=True)
    shift = (offset * weight_sum) // total
    reached = (total * before - shift <= row * weight_sum) & (lane < total)
    ancestor = jnp.sum(reached.astype(jnp.int32), axis=1, keepdims=True) - 1
    ancestor = jnp.broadcast_to(ancestor, (total, lanes))
    return ancestor + jnp.where(ancestor == heavy, 0, total)


def general_kernel(offset_ref, w_ref, out_ref):
    out_ref[...] = entries_of(offset_ref[0], w_ref[...])


def plan_kernel(slots, offset_ref, w_ref, padded_ref, code_ref, found_ref, entry_ref, *piece_refs):
    total, count = w_ref.shape[0], padded_ref.shape[0]
    size = total // count
    entry = entries_of(offset_ref[0], w_ref[...])
    entry_ref[...] = entry
    found = {slot: entry[slot, 0] for slot in slots}
    for n, slot in enumerate(slots):
        found_ref[n] = found[slot]
    last, second = found[total - 1], found[total - 2]
    way = jnp.where(last >= total, 1 + (last - total) // count, 0)
    for slot in slots:
        if slot < total - len(piece_refs):
            way = jnp.where(found[slot] >= total, 1 + size, way)
    code_ref[0] = way + jnp.where(second >= total, (second - total) // count, size) * (1 << FIELD)
    for n, piece_ref in enumerate(piece_refs):
        piece_ref[...] = padded_ref[found[total - 1 - n] % count]


def plan(every_weight, offset, padded, slots, pieces):
    return pl.pallas_call(
        lambda *refs: plan_kernel(slots, *refs),
        out_shape=(shape_of((1,), jnp.int32), shape_of((len(slots),), jnp.int32),
                   shape_of(every_weight.shape, jnp.int32)) + (shape_of(padded.shape[1:]),) * pieces,
        in_specs=[SMEM, VMEM, VMEM],
        out_specs=(SMEM, SMEM, VMEM) + (VMEM,) * pieces,
        compiler_params=LIMIT,
    )(offset, every_weight, padded)


def move_kernel(fields, entry_ref, obs_vmem, heavy_ref, *refs):
    count = len(refs) - 6
    lights, (moved_ref, misfit_ref, work_a, work_b, obs_ref, sem) = refs[:count], refs[count:]
    fetch = pltpu.make_async_copy(obs_vmem, obs_ref, sem)
    fetch.start()
    lons = heavy_ref.shape[1]
    rows = moved_ref.shape[1] // fields
    total, obs = entry_ref.shape[0], obs_ref.shape[1]
    here = lax.axis_index("dom")
    slab, slabs = lax.axis_index("space"), lax.axis_size("space")
    has_low, has_high = slab > 0, slab < slabs - 1
    lanes = lax.broadcasted_iota(jnp.int32, (1, lons), 1)
    work = (work_a, work_b)

    def load(ref):
        for f in range(fields):
            at = fields * rows + 2 * STEPS * f
            work_a[f, pl.ds(PAD, rows), :] = ref[pl.ds(f * rows, rows), :]
            work_a[f, pl.ds(PAD - STEPS, STEPS), :] = ref[pl.ds(at, STEPS), :]
            work_a[f, pl.ds(PAD + rows, STEPS), :] = ref[pl.ds(at + STEPS, STEPS), :]

    def stepped(src, first, length):
        center = [src[f, pl.ds(first, length), :] for f in range(fields)]
        out = []
        for f in range(fields):
            upper = src[f, pl.ds(first + 1, length), :]
            lower = src[f, pl.ds(first - 1, length), :]
            east = pltpu.roll(center[f], lons - 1, 1)
            west = pltpu.roll(center[f], 1, 1)
            transport = center[0] * (east - west) + center[1] * (upper - lower)
            spread = east + west + upper + lower - 4.0 * center[f]
            out.append(center[f] - 0.5 * ADVECT * transport + DIFFUSE * spread)
        return out

    for p in range(count):
        light = entry_ref[here * count + p, 0] >= total

        @pl.when(light)
        def _():
            load(lights[p])

        @pl.when(jnp.logical_not(light))
        def _():
            load(heavy_ref)

        block = 16
        for step in range(STEPS):
            src = work[step % 2]
            last = step == STEPS - 1
            margin = STEPS - 1 - step
            if not last:
                dst = work[(step + 1) % 2]
                low = stepped(src, PAD - margin, margin)
                high = stepped(src, PAD + rows, margin)
                for f in range(fields):
                    dst[f, pl.ds(PAD - margin, margin), :] = jnp.where(has_low, low[f], 0.0)
                    dst[f, pl.ds(PAD + rows, margin), :] = jnp.where(has_high, high[f], 0.0)
            for b in range(0, rows, block):
                new = stepped(src, PAD + b, block)
                for f in range(fields):
                    if last:
                        moved_ref[p, pl.ds(f * rows + b, block), :] = new[f]
                    else:
                        dst[f, pl.ds(PAD + b, block), :] = new[f]
        if p == 0:
            fetch.wait()
        sums = [jnp.zeros((1, lons), jnp.float32)] * 4
        for o in range(obs):
            cell = obs_ref[0, o].astype(jnp.int32)
            row = moved_ref[p, pl.ds((fields - 1) * rows + cell // lons, 1), :]
            gap = row - obs_ref[1, o]
            sums[o % 4] = sums[o % 4] + jnp.where(lanes == cell % lons, obs_ref[2, o] * (gap * gap), 0.0)
        misfit_ref[pl.ds(p, 1), :] = (sums[0] + sums[1]) + (sums[2] + sums[3])


def move(fields, rows, entry, obs, heavy, lights):
    count, lons = len(lights), heavy.shape[1]
    return pl.pallas_call(
        lambda *refs: move_kernel(fields, *refs),
        out_shape=(shape_of((count, fields * rows, lons)), shape_of((count, lons))),
        in_specs=[VMEM] * (3 + count),
        out_specs=(VMEM, VMEM),
        scratch_shapes=[pltpu.VMEM((fields, rows + 2 * PAD, lons), jnp.float32)] * 2
        + [pltpu.SMEM(obs.shape, obs.dtype), pltpu.SemaphoreType.DMA],
        cost_estimate=pl.CostEstimate(flops=40 * count * heavy.size, bytes_accessed=12 * heavy.size, transcendentals=0),
        compiler_params=LIMIT,
    )(entry, obs, heavy, *lights)


def flush_kernel(in_ref, out_ref, sem):
    copy = pltpu.make_async_copy(in_ref, out_ref, sem)
    copy.start()
    copy.wait()


def flushed(moved):
    return pl.pallas_call(
        flush_kernel,
        out_shape=shape_of(moved.shape),
        in_specs=[VMEM],
        out_specs=pl.BlockSpec(memory_space=pl.ANY),
        scratch_shapes=[pltpu.SemaphoreType.DMA],
        cost_estimate=pl.CostEstimate(flops=0, bytes_accessed=16 * moved.size, transcendentals=0),
        compiler_params=LIMIT,
    )(moved)


def gather_step(part, axis, bit):
    size, place = lax.axis_size(axis), lax.axis_index(axis)
    other = lax.ppermute(part, axis, [(i, i ^ bit) for i in range(size)])
    return jnp.where((place & bit) == 0, jnp.concatenate([part, other]), jnp.concatenate([other, part]))


def summed(part, axis):
    size = lax.axis_size(axis)
    bit = 1
    while bit < size:
        part = part + lax.ppermute(part, axis, [(i, i ^ bit) for i in range(size)])
        bit *= 2
    return part


def heavy_step(heavy, size, bit):
    return heavy + lax.ppermute(heavy, "dom", [(i, i + bit) for i in range(size) if i % (2 * bit) < 2])


def light_slots(total):
    most = HEAVY // (4 * total)
    head = (total // 4 - 1) * most
    tail = (total - 1) * most
    first = -(-total * head // (HEAVY + head))
    last = (total * tail * total + (total - 1) * (HEAVY + tail)) // (total * (HEAVY + tail))
    return list(range(total - 1, total - last - 1, -1)) + list(range(first))


def spread_states(obs, weight_rows, offset_draw, padded, core, halo, size, count):
    total = size * count
    slots = light_slots(total)
    last, second = total - 1, total - 2
    pairs = [(i, i ^ 1) for i in range(size)]
    heavy, obs = joined(obs, core, lax.ppermute(core, "dom", pairs[:2]), halo, lax.ppermute(halo, "dom", pairs[:2]))
    weight_rows = gather_step(weight_rows, "dom", 2)
    bit = 4
    while bit < size:
        weight_rows = gather_step(weight_rows, "dom", bit)
        bit *= 2
    code, found, entry, piece, second_piece = plan(weight_rows, offset_draw, padded, slots, 2)
    bit = size // 2
    while bit > 2:
        heavy = heavy_step(heavy, size, bit)
        bit //= 2
    way, other = code[0] & ((1 << FIELD) - 1), code[0] >> FIELD

    def send(part, slot, device):
        target = slot // count
        return part if device == target else lax.ppermute(part, "dom", [(device, target)])

    def maybe(part, slot, index, reach):
        ways = [lambda device=device: send(part, slot, device) for device in range(reach)]
        ways.append(lambda: part)
        return lax.switch(jnp.minimum(index, reach), ways)

    def none():
        return heavy_step(heavy, size, bit), second_piece, piece

    def known(device):
        def run():
            light = send(piece, last, device)
            return heavy_step(heavy, size, bit), maybe(second_piece, second, other, device + 1), light
        return run

    def mixed():
        lights = [second_piece, piece]
        for n, slot in enumerate(slots):
            part = lax.dynamic_index_in_dim(padded, found[n] % count, 0, keepdims=False)
            reach = size if slot >= count else 2
            got = maybe(part, slot, jnp.where(found[n] >= total, (found[n] - total) // count, reach), reach)
            k = slot % count
            lights[k] = jnp.where(lax.axis_index("dom") == slot // count, got, lights[k])
        return (heavy_step(heavy, size, bit), *lights)

    heavy, *lights = lax.switch(way, [none] + [known(d) for d in range(size)] + [mixed])
    return obs, entry, heavy, lights


def local(states, weights, offset_draw, obs_cells, obs_values, obs_precision):
    shape = states.shape
    count, fields, rows, lons = shape
    size = lax.axis_size("dom")
    slabs = lax.axis_size("space")
    total = count * size
    own_rows = jnp.broadcast_to(weights[:, None], (count, max(lons, total)))
    obs = jnp.stack([obs_cells.astype(jnp.float32), obs_values, obs_precision])
    weight_rows = gather_step(own_rows, "dom", 1)
    near, far, states, core = opening(own_rows, states)
    near = lax.ppermute(near, "space", [(i, i ^ 1) for i in range(slabs)])
    far = lax.ppermute(far, "space", [(i, (i + 1 if i % 2 else i - 1) % slabs) for i in range(slabs)])
    padded, halo = padding(own_rows, states, near, far)
    if size <= 8 and count == 2 and total // 4 == 2 * count:
        obs, entry, heavy, lights = spread_states(obs, weight_rows, offset_draw, padded, core, halo, size, count)
    else:
        bit = 2
        while bit < size:
            weight_rows = gather_step(weight_rows, "dom", bit)
            bit *= 2
        entry = pl.pallas_call(
            general_kernel, out_shape=shape_of(weight_rows.shape, jnp.int32), in_specs=[SMEM, VMEM], out_specs=VMEM,
        )(offset_draw, weight_rows) % total
        mine = lax.dynamic_slice_in_dim(entry[:, 0], lax.axis_index("dom") * count, count)
        entry = entry + total
        taken = jnp.take(lax.all_gather(padded, "dom", axis=0, tiled=True), mine, axis=0)
        heavy, lights = taken[0], [taken[k] for k in range(count)]
    out, misfit = move(fields, rows, entry, obs, heavy, lights)
    out = flushed(out)
    misfit = jnp.sum(summed(misfit, "space"), axis=1)
    return out.reshape(shape), -0.5 * misfit / (obs_cells.shape[0] * slabs)


def solution(mesh):
    return jax.shard_map(
        local,
        mesh=mesh,
        in_specs=(P("dom", None, "space", None), P("dom"), P(), P("space"), P("space"), P("space")),
        out_specs=(P("dom", None, "space", None), P("dom")),
        check_vma=False,
    )
```

```python
import jax
import jax.numpy as jnp
from jax import lax
from jax.experimental import pallas as pl
from jax.experimental.pallas import tpu as pltpu
from jax.sharding import PartitionSpec as P

STEPS = 2
ADVECT = 0.25
DIFFUSE = 0.2
HEAVY = 4095
PAD = 8
FIELD = 8
TILE = 8

LIMIT = pltpu.CompilerParams(vmem_limit_bytes=6 * 1024 * 1024)
SMEM = pl.BlockSpec(memory_space=pltpu.SMEM)
VMEM = pl.BlockSpec(memory_space=pltpu.VMEM)


def shape_of(shape, dtype=jnp.float32):
    return jax.ShapeDtypeStruct(shape, dtype)


def halo_rows(fields):
    return -(-2 * STEPS * fields // TILE) * TILE


def open_kernel(w_ref, states_ref, near_ref, far_ref, copy_ref, heavy_ref):
    count, fields, rows, lons = states_ref.shape
    even = lax.axis_index("space") % 2 == 0
    top = states_ref[:, :, pl.ds(0, STEPS), :]
    bottom = states_ref[:, :, pl.ds(rows - STEPS, STEPS), :]
    near_ref[...] = jnp.where(even, bottom, top)
    far_ref[...] = jnp.where(even, top, bottom)
    for f in range(fields):
        for b in range(0, rows, 32):
            block = pl.ds(b, 32)
            whole = jnp.zeros((32, lons), jnp.float32)
            for p in range(count):
                part = states_ref[p, f, block, :]
                copy_ref[p, f, block, :] = part
                whole = jnp.where(w_ref[pl.ds(p, 1), :lons] == HEAVY, part, whole)
            heavy_ref[pl.ds(f * rows + b, 32), :] = whole


def opening(weight_rows, states):
    count, fields, rows, lons = states.shape
    edge = (count, fields, STEPS, lons)
    return pl.pallas_call(
        open_kernel,
        out_shape=(shape_of(edge), shape_of(edge), shape_of(states.shape), shape_of((fields * rows, lons))),
        in_specs=[VMEM, VMEM],
        out_specs=(VMEM,) * 4,
        compiler_params=LIMIT,
    )(weight_rows, states)


def pad_kernel(w_ref, states_ref, near_ref, far_ref, padded_ref, halo_ref):
    count, fields, rows, lons = states_ref.shape
    slab, slabs = lax.axis_index("space"), lax.axis_size("space")
    even = slab % 2 == 0
    extra = halo_ref.shape[0]
    halo_ref[...] = jnp.zeros(halo_ref.shape, jnp.float32)
    for p in range(count):
        for f in range(fields):
            padded_ref[p, pl.ds(f * rows, rows), :] = states_ref[p, f]
        padded_ref[p, pl.ds(fields * rows, extra), :] = jnp.zeros((extra, lons), jnp.float32)
        for f in range(fields):
            near, far = near_ref[p, f], far_ref[p, f]
            below = jnp.where(slab > 0, jnp.where(even, far, near), 0.0)
            above = jnp.where(slab < slabs - 1, jnp.where(even, near, far), 0.0)
            at = fields * rows + 2 * STEPS * f
            padded_ref[p, pl.ds(at, STEPS), :] = below
            padded_ref[p, pl.ds(at + STEPS, STEPS), :] = above
        halo = padded_ref[p, pl.ds(fields * rows, extra), :]
        halo_ref[...] = jnp.where(w_ref[pl.ds(p, 1), :lons] == HEAVY, halo, halo_ref[...])


def padding(weight_rows, states, near, far):
    count, fields, rows, lons = states.shape
    extra = halo_rows(fields)
    return pl.pallas_call(
        pad_kernel,
        out_shape=(shape_of((count, fields * rows + extra, lons)), shape_of((extra, lons))),
        in_specs=[VMEM] * 4,
        out_specs=(VMEM, VMEM),
        compiler_params=LIMIT,
    )(weight_rows, states, near, far)


def join_kernel(obs_ref, core_ref, other_core_ref, halo_ref, other_halo_ref, out_ref, obs_copy_ref):
    obs_copy_ref[...] = obs_ref[...]
    tall, extra = core_ref.shape[0], halo_ref.shape[0]
    out_ref[pl.ds(0, tall), :] = core_ref[...] + other_core_ref[...]
    out_ref[pl.ds(tall, extra), :] = halo_ref[...] + other_halo_ref[...]


def joined(obs, core, other_core, halo, other_halo):
    return pl.pallas_call(
        join_kernel,
        out_shape=(shape_of((core.shape[0] + halo.shape[0], core.shape[1])), shape_of(obs.shape)),
        in_specs=[VMEM] * 5,
        out_specs=(VMEM, VMEM),
        compiler_params=LIMIT,
    )(obs, core, other_core, halo, other_halo)


def entries_of(offset, w):
    total, lanes = w.shape
    row = lax.broadcasted_iota(jnp.int32, (total, lanes), 0)
    lane = lax.broadcasted_iota(jnp.int32, (total, lanes), 1)
    before = jnp.sum(jnp.where(row < lane, w, 0), axis=0, keepdims=True)
    weight_sum = jnp.sum(w, axis=0, keepdims=True)
    heavy = jnp.sum(jnp.where(w == HEAVY, row, 0), axis=0, keepdims=True)
    shift = (offset * weight_sum) // total
    reached = (total * before - shift <= row * weight_sum) & (lane < total)
    ancestor = jnp.sum(reached.astype(jnp.int32), axis=1, keepdims=True) - 1
    ancestor = jnp.broadcast_to(ancestor, (total, lanes))
    return ancestor + jnp.where(ancestor == heavy, 0, total)


def general_kernel(offset_ref, w_ref, out_ref):
    out_ref[...] = entries_of(offset_ref[0], w_ref[...])


def plan_kernel(slots, offset_ref, w_ref, padded_ref, code_ref, found_ref, entry_ref, *piece_refs):
    total, count = w_ref.shape[0], padded_ref.shape[0]
    size = total // count
    entry = entries_of(offset_ref[0], w_ref[...])
    entry_ref[...] = entry
    found = {slot: entry[slot, 0] for slot in slots}
    for n, slot in enumerate(slots):
        found_ref[n] = found[slot]
    last, second = found[total - 1], found[total - 2]
    way = jnp.where(last >= total, 1 + (last - total) // count, 0)
    for slot in slots:
        if slot < total - len(piece_refs):
            remote = (found[slot] >= total) & ((found[slot] - total) // count != slot // count)
            way = jnp.where(remote, 1 + size, way)
    code_ref[0] = way + jnp.where(second >= total, (second - total) // count, size) * (1 << FIELD)
    for n, piece_ref in enumerate(piece_refs):
        piece_ref[...] = padded_ref[found[total - 1 - n] % count]


def plan(every_weight, offset, padded, slots, pieces):
    return pl.pallas_call(
        lambda *refs: plan_kernel(slots, *refs),
        out_shape=(shape_of((1,), jnp.int32), shape_of((len(slots),), jnp.int32),
                   shape_of(every_weight.shape, jnp.int32)) + (shape_of(padded.shape[1:]),) * pieces,
        in_specs=[SMEM, VMEM, VMEM],
        out_specs=(SMEM, SMEM, VMEM) + (VMEM,) * pieces,
        compiler_params=LIMIT,
    )(offset, every_weight, padded)


def move_kernel(fields, entry_ref, obs_vmem, padded_ref, heavy_ref, *refs):
    count = len(refs) - 6
    lights, (moved_ref, misfit_ref, work_a, work_b, obs_ref, sem) = refs[:count], refs[count:]
    fetch = pltpu.make_async_copy(obs_vmem, obs_ref, sem)
    fetch.start()
    lons = heavy_ref.shape[1]
    rows = moved_ref.shape[1] // fields
    total, obs = entry_ref.shape[0], obs_ref.shape[1]
    here = lax.axis_index("dom")
    slab, slabs = lax.axis_index("space"), lax.axis_size("space")
    has_low, has_high = slab > 0, slab < slabs - 1
    lanes = lax.broadcasted_iota(jnp.int32, (1, lons), 1)
    work = (work_a, work_b)

    def load(ref):
        for f in range(fields):
            at = fields * rows + 2 * STEPS * f
            work_a[f, pl.ds(PAD, rows), :] = ref[pl.ds(f * rows, rows), :]
            work_a[f, pl.ds(PAD - STEPS, STEPS), :] = ref[pl.ds(at, STEPS), :]
            work_a[f, pl.ds(PAD + rows, STEPS), :] = ref[pl.ds(at + STEPS, STEPS), :]

    def stepped(src, first, length):
        center = [src[f, pl.ds(first, length), :] for f in range(fields)]
        out = []
        for f in range(fields):
            upper = src[f, pl.ds(first + 1, length), :]
            lower = src[f, pl.ds(first - 1, length), :]
            east = pltpu.roll(center[f], lons - 1, 1)
            west = pltpu.roll(center[f], 1, 1)
            transport = center[0] * (east - west) + center[1] * (upper - lower)
            spread = east + west + upper + lower - 4.0 * center[f]
            out.append(center[f] - 0.5 * ADVECT * transport + DIFFUSE * spread)
        return out

    for p in range(count):
        entry = entry_ref[here * count + p, 0]
        light = entry >= total
        near_by = light & ((entry - total) // count == here)

        @pl.when(near_by)
        def _():
            load(padded_ref.at[entry % count])

        @pl.when(light & jnp.logical_not(near_by))
        def _():
            load(lights[p])

        @pl.when(jnp.logical_not(light))
        def _():
            load(heavy_ref)

        block = 16
        for step in range(STEPS):
            src = work[step % 2]
            last = step == STEPS - 1
            margin = STEPS - 1 - step
            if not last:
                dst = work[(step + 1) % 2]
                low = stepped(src, PAD - margin, margin)
                high = stepped(src, PAD + rows, margin)
                for f in range(fields):
                    dst[f, pl.ds(PAD - margin, margin), :] = jnp.where(has_low, low[f], 0.0)
                    dst[f, pl.ds(PAD + rows, margin), :] = jnp.where(has_high, high[f], 0.0)
            for b in range(0, rows, block):
                new = stepped(src, PAD + b, block)
                for f in range(fields):
                    if last:
                        moved_ref[p, pl.ds(f * rows + b, block), :] = new[f]
                    else:
                        dst[f, pl.ds(PAD + b, block), :] = new[f]
        if p == 0:
            fetch.wait()
        sums = [jnp.zeros((1, lons), jnp.float32)] * 4
        for o in range(obs):
            cell = obs_ref[0, o].astype(jnp.int32)
            row = moved_ref[p, pl.ds((fields - 1) * rows + cell // lons, 1), :]
            gap = row - obs_ref[1, o]
            sums[o % 4] = sums[o % 4] + jnp.where(lanes == cell % lons, obs_ref[2, o] * (gap * gap), 0.0)
        misfit_ref[pl.ds(p, 1), :] = (sums[0] + sums[1]) + (sums[2] + sums[3])


def move(fields, rows, entry, obs, padded, heavy, lights):
    count, lons = len(lights), heavy.shape[1]
    return pl.pallas_call(
        lambda *refs: move_kernel(fields, *refs),
        out_shape=(shape_of((count, fields * rows, lons)), shape_of((count, lons))),
        in_specs=[VMEM] * (4 + count),
        out_specs=(VMEM, VMEM),
        scratch_shapes=[pltpu.VMEM((fields, rows + 2 * PAD, lons), jnp.float32)] * 2
        + [pltpu.SMEM(obs.shape, obs.dtype), pltpu.SemaphoreType.DMA],
        cost_estimate=pl.CostEstimate(flops=40 * count * heavy.size, bytes_accessed=12 * heavy.size, transcendentals=0),
        compiler_params=LIMIT,
    )(entry, obs, padded, heavy, *lights)


def flush_kernel(in_ref, out_ref, sem):
    copy = pltpu.make_async_copy(in_ref, out_ref, sem)
    copy.start()
    copy.wait()


def flushed(moved):
    return pl.pallas_call(
        flush_kernel,
        out_shape=shape_of(moved.shape),
        in_specs=[VMEM],
        out_specs=pl.BlockSpec(memory_space=pl.ANY),
        scratch_shapes=[pltpu.SemaphoreType.DMA],
        cost_estimate=pl.CostEstimate(flops=0, bytes_accessed=16 * moved.size, transcendentals=0),
        compiler_params=LIMIT,
    )(moved)


def gather_step(part, axis, bit):
    size, place = lax.axis_size(axis), lax.axis_index(axis)
    other = lax.ppermute(part, axis, [(i, i ^ bit) for i in range(size)])
    return jnp.where((place & bit) == 0, jnp.concatenate([part, other]), jnp.concatenate([other, part]))


def summed(part, axis):
    size = lax.axis_size(axis)
    bit = 1
    while bit < size:
        part = part + lax.ppermute(part, axis, [(i, i ^ bit) for i in range(size)])
        bit *= 2
    return part


def heavy_step(heavy, size, bit):
    return heavy + lax.ppermute(heavy, "dom", [(i, i + bit) for i in range(size) if i % (2 * bit) < 2])


def light_slots(total):
    most = HEAVY // (4 * total)
    head = (total // 4 - 1) * most
    tail = (total - 1) * most
    first = -(-total * head // (HEAVY + head))
    last = (total * tail * total + (total - 1) * (HEAVY + tail)) // (total * (HEAVY + tail))
    return list(range(total - 1, total - last - 1, -1)) + list(range(first))


def spread_states(obs, weight_rows, offset_draw, padded, core, halo, size, count):
    total = size * count
    slots = light_slots(total)
    last, second = total - 1, total - 2
    pairs = [(i, i ^ 1) for i in range(size)]
    heavy, obs = joined(obs, core, lax.ppermute(core, "dom", pairs[:2]), halo, lax.ppermute(halo, "dom", pairs[:2]))
    weight_rows = gather_step(weight_rows, "dom", 2)
    bit = 4
    while bit < size:
        weight_rows = gather_step(weight_rows, "dom", bit)
        bit *= 2
    code, found, entry, piece, second_piece = plan(weight_rows, offset_draw, padded, slots, 2)
    bit = size // 2
    while bit > 2:
        heavy = heavy_step(heavy, size, bit)
        bit //= 2
    way, other = code[0] & ((1 << FIELD) - 1), code[0] >> FIELD

    def send(part, slot, device):
        target = slot // count
        return part if device == target else lax.ppermute(part, "dom", [(device, target)])

    def maybe(part, slot, index, reach):
        ways = [lambda device=device: send(part, slot, device) for device in range(reach)]
        ways.append(lambda: part)
        return lax.switch(jnp.minimum(index, reach), ways)

    def none():
        return heavy_step(heavy, size, bit), second_piece, piece

    def known(device):
        def run():
            light = send(piece, last, device)
            return heavy_step(heavy, size, bit), maybe(second_piece, second, other, device + 1), light
        return run

    def mixed():
        lights = [second_piece, piece]
        for n, slot in enumerate(slots):
            part = lax.dynamic_index_in_dim(padded, found[n] % count, 0, keepdims=False)
            reach = size if slot >= count else 2
            got = maybe(part, slot, jnp.where(found[n] >= total, (found[n] - total) // count, reach), reach)
            k = slot % count
            lights[k] = jnp.where(lax.axis_index("dom") == slot // count, got, lights[k])
        return (heavy_step(heavy, size, bit), *lights)

    heavy, *lights = lax.switch(way, [none] + [known(d) for d in range(size)] + [mixed])
    return obs, entry, heavy, lights


def local(states, weights, offset_draw, obs_cells, obs_values, obs_precision):
    shape = states.shape
    count, fields, rows, lons = shape
    size = lax.axis_size("dom")
    slabs = lax.axis_size("space")
    total = count * size
    own_rows = jnp.broadcast_to(weights[:, None], (count, max(lons, total)))
    obs = jnp.stack([obs_cells.astype(jnp.float32), obs_values, obs_precision])
    weight_rows = gather_step(own_rows, "dom", 1)
    near, far, states, core = opening(own_rows, states)
    near = lax.ppermute(near, "space", [(i, i ^ 1) for i in range(slabs)])
    far = lax.ppermute(far, "space", [(i, (i + 1 if i % 2 else i - 1) % slabs) for i in range(slabs)])
    padded, halo = padding(own_rows, states, near, far)
    if size <= 8 and count == 2 and total // 4 == 2 * count:
        obs, entry, heavy, lights = spread_states(obs, weight_rows, offset_draw, padded, core, halo, size, count)
    else:
        bit = 2
        while bit < size:
            weight_rows = gather_step(weight_rows, "dom", bit)
            bit *= 2
        entry = pl.pallas_call(
            general_kernel, out_shape=shape_of(weight_rows.shape, jnp.int32), in_specs=[SMEM, VMEM], out_specs=VMEM,
        )(offset_draw, weight_rows) % total
        mine = lax.dynamic_slice_in_dim(entry[:, 0], lax.axis_index("dom") * count, count)
        padded_slots = jnp.arange(total, dtype=jnp.int32)[:, None]
        entry = jnp.broadcast_to(padded_slots + total, entry.shape)
        taken = jnp.take(lax.all_gather(padded, "dom", axis=0, tiled=True), mine, axis=0)
        padded = taken
        heavy, lights = taken[0], [taken[k] for k in range(count)]
    out, misfit = move(fields, rows, entry, obs, padded, heavy, lights)
    out = flushed(out)
    misfit = jnp.sum(summed(misfit, "space"), axis=1)
    return out.reshape(shape), -0.5 * misfit / (obs_cells.shape[0] * slabs)


def solution(mesh):
    return jax.shard_map(
        local,
        mesh=mesh,
        in_specs=(P("dom", None, "space", None), P("dom"), P(), P("space"), P("space"), P("space")),
        out_specs=(P("dom", None, "space", None), P("dom")),
        check_vma=False,
    )
```

```python
import jax
import jax.numpy as jnp
from jax import lax
from jax.experimental import pallas as pl
from jax.experimental.pallas import tpu as pltpu
from jax.sharding import PartitionSpec as P

STEPS = 2
ADVECT = 0.25
DIFFUSE = 0.2
HEAVY = 4095
PAD = 8
FIELD = 8
TILE = 8

LIMIT = pltpu.CompilerParams(vmem_limit_bytes=6 * 1024 * 1024)
SMEM = pl.BlockSpec(memory_space=pltpu.SMEM)
VMEM = pl.BlockSpec(memory_space=pltpu.VMEM)


def shape_of(shape, dtype=jnp.float32):
    return jax.ShapeDtypeStruct(shape, dtype)


def halo_rows(fields):
    return -(-2 * STEPS * fields // TILE) * TILE


def open_kernel(w_ref, states_ref, near_ref, far_ref, copy_ref, heavy_ref):
    count, fields, rows, lons = states_ref.shape
    even = lax.axis_index("space") % 2 == 0
    top = states_ref[:, :, pl.ds(0, STEPS), :]
    bottom = states_ref[:, :, pl.ds(rows - STEPS, STEPS), :]
    near_ref[...] = jnp.where(even, bottom, top)
    far_ref[...] = jnp.where(even, top, bottom)
    for f in range(fields):
        for b in range(0, rows, 32):
            block = pl.ds(b, 32)
            whole = jnp.zeros((32, lons), jnp.float32)
            for p in range(count):
                part = states_ref[p, f, block, :]
                copy_ref[p, f, block, :] = part
                whole = jnp.where(w_ref[pl.ds(p, 1), :lons] == HEAVY, part, whole)
            heavy_ref[pl.ds(f * rows + b, 32), :] = whole


def opening(weight_rows, states):
    count, fields, rows, lons = states.shape
    edge = (count, fields, STEPS, lons)
    return pl.pallas_call(
        open_kernel,
        out_shape=(shape_of(edge), shape_of(edge), shape_of(states.shape), shape_of((fields * rows, lons))),
        in_specs=[VMEM, VMEM],
        out_specs=(VMEM,) * 4,
        compiler_params=LIMIT,
    )(weight_rows, states)


def pad_kernel(w_ref, states_ref, near_ref, far_ref, padded_ref, halo_ref):
    count, fields, rows, lons = states_ref.shape
    slab, slabs = lax.axis_index("space"), lax.axis_size("space")
    even = slab % 2 == 0
    extra = halo_ref.shape[0]
    halo_ref[...] = jnp.zeros(halo_ref.shape, jnp.float32)
    for p in range(count):
        for f in range(fields):
            padded_ref[p, pl.ds(f * rows, rows), :] = states_ref[p, f]
        padded_ref[p, pl.ds(fields * rows, extra), :] = jnp.zeros((extra, lons), jnp.float32)
        for f in range(fields):
            near, far = near_ref[p, f], far_ref[p, f]
            below = jnp.where(slab > 0, jnp.where(even, far, near), 0.0)
            above = jnp.where(slab < slabs - 1, jnp.where(even, near, far), 0.0)
            at = fields * rows + 2 * STEPS * f
            padded_ref[p, pl.ds(at, STEPS), :] = below
            padded_ref[p, pl.ds(at + STEPS, STEPS), :] = above
        halo = padded_ref[p, pl.ds(fields * rows, extra), :]
        halo_ref[...] = jnp.where(w_ref[pl.ds(p, 1), :lons] == HEAVY, halo, halo_ref[...])


def padding(weight_rows, states, near, far):
    count, fields, rows, lons = states.shape
    extra = halo_rows(fields)
    return pl.pallas_call(
        pad_kernel,
        out_shape=(shape_of((count, fields * rows + extra, lons)), shape_of((extra, lons))),
        in_specs=[VMEM] * 4,
        out_specs=(VMEM, VMEM),
        compiler_params=LIMIT,
    )(weight_rows, states, near, far)


def join_kernel(obs_ref, core_ref, other_core_ref, halo_ref, other_halo_ref, out_ref, obs_copy_ref):
    obs_copy_ref[...] = obs_ref[...]
    tall, extra = core_ref.shape[0], halo_ref.shape[0]
    out_ref[pl.ds(0, tall), :] = core_ref[...] + other_core_ref[...]
    out_ref[pl.ds(tall, extra), :] = halo_ref[...] + other_halo_ref[...]


def joined(obs, core, other_core, halo, other_halo):
    return pl.pallas_call(
        join_kernel,
        out_shape=(shape_of((core.shape[0] + halo.shape[0], core.shape[1])), shape_of(obs.shape)),
        in_specs=[VMEM] * 5,
        out_specs=(VMEM, VMEM),
        compiler_params=LIMIT,
    )(obs, core, other_core, halo, other_halo)


def entries_of(offset, w):
    total, lanes = w.shape
    row = lax.broadcasted_iota(jnp.int32, (total, lanes), 0)
    lane = lax.broadcasted_iota(jnp.int32, (total, lanes), 1)
    before = jnp.sum(jnp.where(row < lane, w, 0), axis=0, keepdims=True)
    weight_sum = jnp.sum(w, axis=0, keepdims=True)
    heavy = jnp.sum(jnp.where(w == HEAVY, row, 0), axis=0, keepdims=True)
    shift = (offset * weight_sum) // total
    reached = (total * before - shift <= row * weight_sum) & (lane < total)
    ancestor = jnp.sum(reached.astype(jnp.int32), axis=1, keepdims=True) - 1
    ancestor = jnp.broadcast_to(ancestor, (total, lanes))
    return ancestor + jnp.where(ancestor == heavy, 0, total)


def general_kernel(offset_ref, w_ref, out_ref):
    out_ref[...] = entries_of(offset_ref[0], w_ref[...])


def plan_kernel(slots, offset_ref, w_ref, padded_ref, code_ref, found_ref, entry_ref, *piece_refs):
    total, count = w_ref.shape[0], padded_ref.shape[0]
    size = total // count
    entry = entries_of(offset_ref[0], w_ref[...])
    entry_ref[...] = entry
    found = {slot: entry[slot, 0] for slot in slots}
    for n, slot in enumerate(slots):
        found_ref[n] = found[slot]
    last, second = found[total - 1], found[total - 2]
    way = jnp.where(last >= total, 1 + (last - total) // count, 0)
    for slot in slots:
        if slot < total - len(piece_refs):
            remote = (found[slot] >= total) & ((found[slot] - total) // count != slot // count)
            way = jnp.where(remote, 1 + size, way)
    code_ref[0] = way + jnp.where(second >= total, (second - total) // count, size) * (1 << FIELD)
    for n, piece_ref in enumerate(piece_refs):
        piece_ref[...] = padded_ref[found[total - 1 - n] % count]


def plan(every_weight, offset, padded, slots, pieces):
    return pl.pallas_call(
        lambda *refs: plan_kernel(slots, *refs),
        out_shape=(shape_of((1,), jnp.int32), shape_of((len(slots),), jnp.int32),
                   shape_of(every_weight.shape, jnp.int32)) + (shape_of(padded.shape[1:]),) * pieces,
        in_specs=[SMEM, VMEM, VMEM],
        out_specs=(SMEM, SMEM, VMEM) + (VMEM,) * pieces,
        compiler_params=LIMIT,
    )(offset, every_weight, padded)


def move_kernel(fields, entry_ref, obs_vmem, padded_ref, heavy_ref, *refs):
    count = len(refs) - 6
    lights, (moved_ref, misfit_ref, work_a, work_b, obs_ref, sem) = refs[:count], refs[count:]
    fetch = pltpu.make_async_copy(obs_vmem, obs_ref, sem)
    fetch.start()
    lons = heavy_ref.shape[1]
    rows = moved_ref.shape[1] // fields
    total, obs = entry_ref.shape[0], obs_ref.shape[1]
    here = lax.axis_index("dom")
    slab, slabs = lax.axis_index("space"), lax.axis_size("space")
    has_low, has_high = slab > 0, slab < slabs - 1
    lanes = lax.broadcasted_iota(jnp.int32, (1, lons), 1)
    work = (work_a, work_b)

    def load(ref):
        for f in range(fields):
            at = fields * rows + 2 * STEPS * f
            work_a[f, pl.ds(PAD, rows), :] = ref[pl.ds(f * rows, rows), :]
            work_a[f, pl.ds(PAD - STEPS, STEPS), :] = ref[pl.ds(at, STEPS), :]
            work_a[f, pl.ds(PAD + rows, STEPS), :] = ref[pl.ds(at + STEPS, STEPS), :]

    def stepped(src, first, length):
        center = [src[f, pl.ds(first, length), :] for f in range(fields)]
        out = []
        for f in range(fields):
            upper = src[f, pl.ds(first + 1, length), :]
            lower = src[f, pl.ds(first - 1, length), :]
            east = pltpu.roll(center[f], lons - 1, 1)
            west = pltpu.roll(center[f], 1, 1)
            transport = center[0] * (east - west) + center[1] * (upper - lower)
            spread = east + west + upper + lower - 4.0 * center[f]
            out.append(center[f] - 0.5 * ADVECT * transport + DIFFUSE * spread)
        return out

    for p in range(count):
        entry = entry_ref[here * count + p, 0]
        light = entry >= total
        near_by = light & ((entry - total) // count == here)

        @pl.when(near_by)
        def _():
            load(padded_ref.at[entry % count])

        @pl.when(light & jnp.logical_not(near_by))
        def _():
            load(lights[p])

        @pl.when(jnp.logical_not(light))
        def _():
            load(heavy_ref)

        block = 16
        for step in range(STEPS):
            src = work[step % 2]
            last = step == STEPS - 1
            margin = STEPS - 1 - step
            if not last:
                dst = work[(step + 1) % 2]
                low = stepped(src, PAD - margin, margin)
                high = stepped(src, PAD + rows, margin)
                for f in range(fields):
                    dst[f, pl.ds(PAD - margin, margin), :] = jnp.where(has_low, low[f], 0.0)
                    dst[f, pl.ds(PAD + rows, margin), :] = jnp.where(has_high, high[f], 0.0)
            for b in range(0, rows, block):
                new = stepped(src, PAD + b, block)
                for f in range(fields):
                    if last:
                        moved_ref[p, pl.ds(f * rows + b, block), :] = new[f]
                    else:
                        dst[f, pl.ds(PAD + b, block), :] = new[f]
        if p == 0:
            fetch.wait()
        sums = [jnp.zeros((1, lons), jnp.float32)] * 4
        for o in range(obs):
            cell = obs_ref[0, o].astype(jnp.int32)
            row = moved_ref[p, pl.ds((fields - 1) * rows + cell // lons, 1), :]
            gap = row - obs_ref[1, o]
            sums[o % 4] = sums[o % 4] + jnp.where(lanes == cell % lons, obs_ref[2, o] * (gap * gap), 0.0)
        misfit_ref[pl.ds(p, 1), :] = (sums[0] + sums[1]) + (sums[2] + sums[3])


def move(fields, rows, entry, obs, padded, heavy, lights):
    count, lons = len(lights), heavy.shape[1]
    return pl.pallas_call(
        lambda *refs: move_kernel(fields, *refs),
        out_shape=(shape_of((count, fields * rows, lons)), shape_of((count, lons))),
        in_specs=[VMEM] * (4 + count),
        out_specs=(VMEM, VMEM),
        scratch_shapes=[pltpu.VMEM((fields, rows + 2 * PAD, lons), jnp.float32)] * 2
        + [pltpu.SMEM(obs.shape, obs.dtype), pltpu.SemaphoreType.DMA],
        cost_estimate=pl.CostEstimate(flops=40 * count * heavy.size, bytes_accessed=12 * heavy.size, transcendentals=0),
        compiler_params=LIMIT,
    )(entry, obs, padded, heavy, *lights)


def flush_kernel(in_ref, out_ref, sem):
    copy = pltpu.make_async_copy(in_ref, out_ref, sem)
    copy.start()
    copy.wait()


def flushed(moved):
    return pl.pallas_call(
        flush_kernel,
        out_shape=shape_of(moved.shape),
        in_specs=[VMEM],
        out_specs=pl.BlockSpec(memory_space=pl.ANY),
        scratch_shapes=[pltpu.SemaphoreType.DMA],
        cost_estimate=pl.CostEstimate(flops=0, bytes_accessed=16 * moved.size, transcendentals=0),
        compiler_params=LIMIT,
    )(moved)


def gather_step(part, axis, bit):
    size, place = lax.axis_size(axis), lax.axis_index(axis)
    other = lax.ppermute(part, axis, [(i, i ^ bit) for i in range(size)])
    return jnp.where((place & bit) == 0, jnp.concatenate([part, other]), jnp.concatenate([other, part]))


def summed(part, axis):
    size = lax.axis_size(axis)
    parts = [part] + [lax.ppermute(part, axis, [(i, i ^ k) for i in range(size)]) for k in range(1, size)]
    while len(parts) > 1:
        parts = [a + b for a, b in zip(parts[::2], parts[1::2])]
    return parts[0]


def heavy_step(heavy, size, bit):
    return heavy + lax.ppermute(heavy, "dom", [(i, i + bit) for i in range(size) if i % (2 * bit) < 2])


def light_slots(total):
    most = HEAVY // (4 * total)
    head = (total // 4 - 1) * most
    tail = (total - 1) * most
    first = -(-total * head // (HEAVY + head))
    last = (total * tail * total + (total - 1) * (HEAVY + tail)) // (total * (HEAVY + tail))
    return list(range(total - 1, total - last - 1, -1)) + list(range(first))


def spread_states(obs, weight_rows, offset_draw, padded, core, halo, size, count):
    total = size * count
    slots = light_slots(total)
    last, second = total - 1, total - 2
    pairs = [(i, i ^ 1) for i in range(size)]
    heavy, obs = joined(obs, core, lax.ppermute(core, "dom", pairs[:2]), halo, lax.ppermute(halo, "dom", pairs))
    weight_rows = gather_step(weight_rows, "dom", 2)
    bit = 4
    while bit < size:
        weight_rows = gather_step(weight_rows, "dom", bit)
        bit *= 2
    code, found, entry, piece, second_piece = plan(weight_rows, offset_draw, padded, slots, 2)
    bit = size // 2
    while bit > 2:
        heavy = heavy_step(heavy, size, bit)
        bit //= 2
    way, other = code[0] & ((1 << FIELD) - 1), code[0] >> FIELD

    def send(part, slot, device):
        target = slot // count
        return part if device == target else lax.ppermute(part, "dom", [(device, target)])

    def maybe(part, slot, index, reach):
        ways = [lambda device=device: send(part, slot, device) for device in range(reach)]
        ways.append(lambda: part)
        return lax.switch(jnp.minimum(index, reach), ways)

    def none():
        return heavy_step(heavy, size, bit), second_piece, piece

    def known(device):
        def run():
            light = send(piece, last, device)
            return heavy_step(heavy, size, bit), maybe(second_piece, second, other, device + 1), light
        return run

    def mixed():
        lights = [second_piece, piece]
        for n, slot in enumerate(slots):
            part = lax.dynamic_index_in_dim(padded, found[n] % count, 0, keepdims=False)
            reach = size if slot >= count else 2
            got = maybe(part, slot, jnp.where(found[n] >= total, (found[n] - total) // count, reach), reach)
            k = slot % count
            lights[k] = jnp.where(lax.axis_index("dom") == slot // count, got, lights[k])
        return (heavy_step(heavy, size, bit), *lights)

    heavy, *lights = lax.switch(way, [none] + [known(d) for d in range(size)] + [mixed])
    return obs, entry, heavy, lights


def local(states, weights, offset_draw, obs_cells, obs_values, obs_precision):
    shape = states.shape
    count, fields, rows, lons = shape
    size = lax.axis_size("dom")
    slabs = lax.axis_size("space")
    total = count * size
    own_rows = jnp.broadcast_to(weights[:, None], (count, max(lons, total)))
    obs = jnp.stack([obs_cells.astype(jnp.float32), obs_values, obs_precision])
    weight_rows = gather_step(own_rows, "dom", 1)
    near, far, states, core = opening(own_rows, states)
    near = lax.ppermute(near, "space", [(i, i ^ 1) for i in range(slabs)])
    far = lax.ppermute(far, "space", [(i, (i + 1 if i % 2 else i - 1) % slabs) for i in range(slabs)])
    padded, halo = padding(own_rows, states, near, far)
    if size <= 8 and count == 2 and total // 4 == 2 * count:
        obs, entry, heavy, lights = spread_states(obs, weight_rows, offset_draw, padded, core, halo, size, count)
    else:
        bit = 2
        while bit < size:
            weight_rows = gather_step(weight_rows, "dom", bit)
            bit *= 2
        entry = pl.pallas_call(
            general_kernel, out_shape=shape_of(weight_rows.shape, jnp.int32), in_specs=[SMEM, VMEM], out_specs=VMEM,
        )(offset_draw, weight_rows) % total
        mine = lax.dynamic_slice_in_dim(entry[:, 0], lax.axis_index("dom") * count, count)
        padded_slots = jnp.arange(total, dtype=jnp.int32)[:, None]
        entry = jnp.broadcast_to(padded_slots + total, entry.shape)
        taken = jnp.take(lax.all_gather(padded, "dom", axis=0, tiled=True), mine, axis=0)
        padded = taken
        heavy, lights = taken[0], [taken[k] for k in range(count)]
    out, misfit = move(fields, rows, entry, obs, padded, heavy, lights)
    out = flushed(out)
    misfit = jnp.sum(summed(misfit, "space"), axis=1)
    return out.reshape(shape), -0.5 * misfit / (obs_cells.shape[0] * slabs)


def solution(mesh):
    return jax.shard_map(
        local,
        mesh=mesh,
        in_specs=(P("dom", None, "space", None), P("dom"), P(), P("space"), P("space"), P("space")),
        out_specs=(P("dom", None, "space", None), P("dom")),
        check_vma=False,
    )
```

```python
import jax
import jax.numpy as jnp
from jax import lax
from jax.experimental import pallas as pl
from jax.experimental.pallas import tpu as pltpu
from jax.sharding import PartitionSpec as P

STEPS = 2
ADVECT = 0.25
DIFFUSE = 0.2
HEAVY = 4095
PAD = 8
FIELD = 8
TILE = 8

LIMIT = pltpu.CompilerParams(vmem_limit_bytes=6 * 1024 * 1024)
SMEM = pl.BlockSpec(memory_space=pltpu.SMEM)
VMEM = pl.BlockSpec(memory_space=pltpu.VMEM)


def shape_of(shape, dtype=jnp.float32):
    return jax.ShapeDtypeStruct(shape, dtype)


def halo_rows(fields):
    return -(-2 * STEPS * fields // TILE) * TILE


def open_kernel(w_ref, states_ref, near_ref, far_ref, copy_ref, heavy_ref):
    count, fields, rows, lons = states_ref.shape
    even = lax.axis_index("space") % 2 == 0
    top = states_ref[:, :, pl.ds(0, STEPS), :]
    bottom = states_ref[:, :, pl.ds(rows - STEPS, STEPS), :]
    near_ref[...] = jnp.where(even, bottom, top)
    far_ref[...] = jnp.where(even, top, bottom)
    for f in range(fields):
        for b in range(0, rows, 32):
            block = pl.ds(b, 32)
            whole = jnp.zeros((32, lons), jnp.float32)
            for p in range(count):
                part = states_ref[p, f, block, :]
                copy_ref[p, f, block, :] = part
                whole = jnp.where(w_ref[pl.ds(p, 1), :lons] == HEAVY, part, whole)
            heavy_ref[pl.ds(f * rows + b, 32), :] = whole


def opening(weight_rows, states):
    count, fields, rows, lons = states.shape
    edge = (count, fields, STEPS, lons)
    return pl.pallas_call(
        open_kernel,
        out_shape=(shape_of(edge), shape_of(edge), shape_of(states.shape), shape_of((fields * rows, lons))),
        in_specs=[VMEM, VMEM],
        out_specs=(VMEM,) * 4,
        compiler_params=LIMIT,
    )(weight_rows, states)


def pad_kernel(w_ref, states_ref, near_ref, far_ref, padded_ref, halo_ref):
    count, fields, rows, lons = states_ref.shape
    slab, slabs = lax.axis_index("space"), lax.axis_size("space")
    even = slab % 2 == 0
    extra = halo_ref.shape[0]
    halo_ref[...] = jnp.zeros(halo_ref.shape, jnp.float32)
    for p in range(count):
        for f in range(fields):
            padded_ref[p, pl.ds(f * rows, rows), :] = states_ref[p, f]
        padded_ref[p, pl.ds(fields * rows, extra), :] = jnp.zeros((extra, lons), jnp.float32)
        for f in range(fields):
            near, far = near_ref[p, f], far_ref[p, f]
            below = jnp.where(slab > 0, jnp.where(even, far, near), 0.0)
            above = jnp.where(slab < slabs - 1, jnp.where(even, near, far), 0.0)
            at = fields * rows + 2 * STEPS * f
            padded_ref[p, pl.ds(at, STEPS), :] = below
            padded_ref[p, pl.ds(at + STEPS, STEPS), :] = above
        halo = padded_ref[p, pl.ds(fields * rows, extra), :]
        halo_ref[...] = jnp.where(w_ref[pl.ds(p, 1), :lons] == HEAVY, halo, halo_ref[...])


def padding(weight_rows, states, near, far):
    count, fields, rows, lons = states.shape
    extra = halo_rows(fields)
    return pl.pallas_call(
        pad_kernel,
        out_shape=(shape_of((count, fields * rows + extra, lons)), shape_of((extra, lons))),
        in_specs=[VMEM] * 4,
        out_specs=(VMEM, VMEM),
        compiler_params=LIMIT,
    )(weight_rows, states, near, far)


def join_kernel(obs_ref, core_ref, other_core_ref, halo_ref, other_halo_ref, out_ref, obs_copy_ref):
    obs_copy_ref[...] = obs_ref[...]
    tall, extra = core_ref.shape[0], halo_ref.shape[0]
    out_ref[pl.ds(0, tall), :] = core_ref[...] + other_core_ref[...]
    out_ref[pl.ds(tall, extra), :] = halo_ref[...] + other_halo_ref[...]


def joined(obs, core, other_core, halo, other_halo):
    return pl.pallas_call(
        join_kernel,
        out_shape=(shape_of((core.shape[0] + halo.shape[0], core.shape[1])), shape_of(obs.shape)),
        in_specs=[VMEM] * 5,
        out_specs=(VMEM, VMEM),
        compiler_params=LIMIT,
    )(obs, core, other_core, halo, other_halo)


def entries_of(offset, w):
    total, lanes = w.shape
    row = lax.broadcasted_iota(jnp.int32, (total, lanes), 0)
    lane = lax.broadcasted_iota(jnp.int32, (total, lanes), 1)
    before = jnp.sum(jnp.where(row < lane, w, 0), axis=0, keepdims=True)
    weight_sum = jnp.sum(w, axis=0, keepdims=True)
    heavy = jnp.sum(jnp.where(w == HEAVY, row, 0), axis=0, keepdims=True)
    shift = (offset * weight_sum) // total
    reached = (total * before - shift <= row * weight_sum) & (lane < total)
    ancestor = jnp.sum(reached.astype(jnp.int32), axis=1, keepdims=True) - 1
    ancestor = jnp.broadcast_to(ancestor, (total, lanes))
    return ancestor + jnp.where(ancestor == heavy, 0, total)


def general_kernel(offset_ref, w_ref, out_ref):
    out_ref[...] = entries_of(offset_ref[0], w_ref[...])


def plan_kernel(slots, offset_ref, w_ref, padded_ref, code_ref, found_ref, entry_ref, *piece_refs):
    total, count = w_ref.shape[0], padded_ref.shape[0]
    size = total // count
    entry = entries_of(offset_ref[0], w_ref[...])
    entry_ref[...] = entry
    found = {slot: entry[slot, 0] for slot in slots}
    for n, slot in enumerate(slots):
        found_ref[n] = found[slot]
    last, second = found[total - 1], found[total - 2]
    way = jnp.where(last >= total, 1 + (last - total) // count, 0)
    for slot in slots:
        if slot < total - len(piece_refs):
            remote = (found[slot] >= total) & ((found[slot] - total) // count != slot // count)
            way = jnp.where(remote, 1 + size, way)
    code_ref[0] = way + jnp.where(second >= total, (second - total) // count, size) * (1 << FIELD)
    for n, piece_ref in enumerate(piece_refs):
        piece_ref[...] = padded_ref[found[total - 1 - n] % count]


def plan(every_weight, offset, padded, slots, pieces):
    return pl.pallas_call(
        lambda *refs: plan_kernel(slots, *refs),
        out_shape=(shape_of((1,), jnp.int32), shape_of((len(slots),), jnp.int32),
                   shape_of(every_weight.shape, jnp.int32)) + (shape_of(padded.shape[1:]),) * pieces,
        in_specs=[SMEM, VMEM, VMEM],
        out_specs=(SMEM, SMEM, VMEM) + (VMEM,) * pieces,
        compiler_params=LIMIT,
    )(offset, every_weight, padded)


def move_kernel(fields, entry_ref, obs_vmem, padded_ref, heavy_ref, *refs):
    count = len(refs) - 6
    lights, (moved_ref, misfit_ref, work_a, work_b, obs_ref, sem) = refs[:count], refs[count:]
    fetch = pltpu.make_async_copy(obs_vmem, obs_ref, sem)
    fetch.start()
    lons = heavy_ref.shape[1]
    rows = moved_ref.shape[1] // fields
    total, obs = entry_ref.shape[0], obs_ref.shape[1]
    here = lax.axis_index("dom")
    slab, slabs = lax.axis_index("space"), lax.axis_size("space")
    has_low, has_high = slab > 0, slab < slabs - 1
    lanes = lax.broadcasted_iota(jnp.int32, (1, lons), 1)
    work = (work_a, work_b)

    def load(ref):
        for f in range(fields):
            at = fields * rows + 2 * STEPS * f
            work_a[f, pl.ds(PAD, rows), :] = ref[pl.ds(f * rows, rows), :]
            work_a[f, pl.ds(PAD - STEPS, STEPS), :] = ref[pl.ds(at, STEPS), :]
            work_a[f, pl.ds(PAD + rows, STEPS), :] = ref[pl.ds(at + STEPS, STEPS), :]

    def stepped(src, first, length):
        center = [src[f, pl.ds(first, length), :] for f in range(fields)]
        out = []
        for f in range(fields):
            upper = src[f, pl.ds(first + 1, length), :]
            lower = src[f, pl.ds(first - 1, length), :]
            east = pltpu.roll(center[f], lons - 1, 1)
            west = pltpu.roll(center[f], 1, 1)
            transport = center[0] * (east - west) + center[1] * (upper - lower)
            spread = east + west + upper + lower - 4.0 * center[f]
            out.append(center[f] - 0.5 * ADVECT * transport + DIFFUSE * spread)
        return out

    for p in range(count):
        entry = entry_ref[here * count + p, 0]
        light = entry >= total
        near_by = light & ((entry - total) // count == here)

        @pl.when(near_by)
        def _():
            load(padded_ref.at[entry % count])

        @pl.when(light & jnp.logical_not(near_by))
        def _():
            load(lights[p])

        @pl.when(jnp.logical_not(light))
        def _():
            load(heavy_ref)

        block = 16
        for step in range(STEPS):
            src = work[step % 2]
            last = step == STEPS - 1
            margin = STEPS - 1 - step
            if not last:
                dst = work[(step + 1) % 2]
                low = stepped(src, PAD - margin, margin)
                high = stepped(src, PAD + rows, margin)
                for f in range(fields):
                    dst[f, pl.ds(PAD - margin, margin), :] = jnp.where(has_low, low[f], 0.0)
                    dst[f, pl.ds(PAD + rows, margin), :] = jnp.where(has_high, high[f], 0.0)
            for b in range(0, rows, block):
                new = stepped(src, PAD + b, block)
                for f in range(fields):
                    if last:
                        moved_ref[p, pl.ds(f * rows + b, block), :] = new[f]
                    else:
                        dst[f, pl.ds(PAD + b, block), :] = new[f]
        if p == 0:
            fetch.wait()
        sums = [jnp.zeros((1, lons), jnp.float32)] * 4
        for o in range(obs):
            cell = obs_ref[0, o].astype(jnp.int32)
            row = moved_ref[p, pl.ds((fields - 1) * rows + cell // lons, 1), :]
            gap = row - obs_ref[1, o]
            sums[o % 4] = sums[o % 4] + jnp.where(lanes == cell % lons, obs_ref[2, o] * (gap * gap), 0.0)
        misfit_ref[pl.ds(p, 1), :] = (sums[0] + sums[1]) + (sums[2] + sums[3])


def move(fields, rows, entry, obs, padded, heavy, lights):
    count, lons = len(lights), heavy.shape[1]
    return pl.pallas_call(
        lambda *refs: move_kernel(fields, *refs),
        out_shape=(shape_of((count, fields * rows, lons)), shape_of((count, lons))),
        in_specs=[VMEM] * (4 + count),
        out_specs=(VMEM, VMEM),
        scratch_shapes=[pltpu.VMEM((fields, rows + 2 * PAD, lons), jnp.float32)] * 2
        + [pltpu.SMEM(obs.shape, obs.dtype), pltpu.SemaphoreType.DMA],
        cost_estimate=pl.CostEstimate(flops=40 * count * heavy.size, bytes_accessed=12 * heavy.size, transcendentals=0),
        compiler_params=LIMIT,
    )(entry, obs, padded, heavy, *lights)


def flush_kernel(in_ref, out_ref, sem):
    copy = pltpu.make_async_copy(in_ref, out_ref, sem)
    copy.start()
    copy.wait()


def flushed(moved):
    return pl.pallas_call(
        flush_kernel,
        out_shape=shape_of(moved.shape),
        in_specs=[VMEM],
        out_specs=pl.BlockSpec(memory_space=pl.ANY),
        scratch_shapes=[pltpu.SemaphoreType.DMA],
        cost_estimate=pl.CostEstimate(flops=0, bytes_accessed=16 * moved.size, transcendentals=0),
        compiler_params=LIMIT,
    )(moved)


def gather_step(part, axis, bit):
    size, place = lax.axis_size(axis), lax.axis_index(axis)
    other = lax.ppermute(part, axis, [(i, i ^ bit) for i in range(size)])
    return jnp.where((place & bit) == 0, jnp.concatenate([part, other]), jnp.concatenate([other, part]))


def summed(part, axis):
    size = lax.axis_size(axis)
    parts = [part] + [lax.ppermute(part, axis, [(i, i ^ k) for i in range(size)]) for k in range(1, size)]
    while len(parts) > 1:
        parts = [a + b for a, b in zip(parts[::2], parts[1::2])]
    return parts[0]


def heavy_step(heavy, size, bit):
    return heavy + lax.ppermute(heavy, "dom", [(i, i + bit) for i in range(size) if i % (2 * bit) < 2])


def light_slots(total):
    most = HEAVY // (4 * total)
    head = (total // 4 - 1) * most
    tail = (total - 1) * most
    first = -(-total * head // (HEAVY + head))
    last = (total * tail * total + (total - 1) * (HEAVY + tail)) // (total * (HEAVY + tail))
    return list(range(total - 1, total - last - 1, -1)) + list(range(first))


def spread_states(obs, weight_rows, offset_draw, padded, core, halo, size, count):
    total = size * count
    slots = light_slots(total)
    last, second = total - 1, total - 2
    pairs = [(i, i ^ 1) for i in range(size)]
    heavy, obs = joined(obs, core, lax.ppermute(core, "dom", pairs[:2]), halo, lax.ppermute(halo, "dom", pairs))
    weight_rows = gather_step(weight_rows, "dom", 2)
    bit = 4
    while bit < size:
        weight_rows = gather_step(weight_rows, "dom", bit)
        bit *= 2
    code, found, entry, piece, second_piece = plan(weight_rows, offset_draw, padded, slots, 2)
    bit = size // 2
    while bit > 2:
        heavy = heavy_step(heavy, size, bit)
        bit //= 2
    way, other = code[0] & ((1 << FIELD) - 1), code[0] >> FIELD

    def send(part, slot, device):
        target = slot // count
        return part if device == target else lax.ppermute(part, "dom", [(device, target)])

    def maybe(part, slot, index, reach):
        ways = [lambda device=device: send(part, slot, device) for device in range(reach)]
        ways.append(lambda: part)
        return lax.switch(jnp.minimum(index, reach), ways)

    def none():
        return heavy_step(heavy, size, bit), second_piece, piece

    def known(device):
        def run():
            light = send(piece, last, device)
            return heavy_step(heavy, size, bit), maybe(second_piece, second, other, device + 1), light
        return run

    def mixed():
        lights = [second_piece, piece]
        ready = {last: piece, second: second_piece}
        for n, slot in enumerate(slots):
            if slot in ready:
                part = ready[slot]
            else:
                part = lax.dynamic_index_in_dim(padded, found[n] % count, 0, keepdims=False)
            reach = size if slot >= count else 2
            got = maybe(part, slot, jnp.where(found[n] >= total, (found[n] - total) // count, reach), reach)
            k = slot % count
            lights[k] = got if slot in ready else jnp.where(lax.axis_index("dom") == slot // count, got, lights[k])
        return (heavy_step(heavy, size, bit), *lights)

    heavy, *lights = lax.switch(way, [none] + [known(d) for d in range(size)] + [mixed])
    return obs, entry, heavy, lights


def local(states, weights, offset_draw, obs_cells, obs_values, obs_precision):
    shape = states.shape
    count, fields, rows, lons = shape
    size = lax.axis_size("dom")
    slabs = lax.axis_size("space")
    total = count * size
    own_rows = jnp.broadcast_to(weights[:, None], (count, max(lons, total)))
    obs = jnp.stack([obs_cells.astype(jnp.float32), obs_values, obs_precision])
    weight_rows = gather_step(own_rows, "dom", 1)
    near, far, states, core = opening(own_rows, states)
    near = lax.ppermute(near, "space", [(i, i ^ 1) for i in range(slabs)])
    far = lax.ppermute(far, "space", [(i, (i + 1 if i % 2 else i - 1) % slabs) for i in range(slabs)])
    padded, halo = padding(own_rows, states, near, far)
    if size <= 8 and count == 2 and total // 4 == 2 * count:
        obs, entry, heavy, lights = spread_states(obs, weight_rows, offset_draw, padded, core, halo, size, count)
    else:
        bit = 2
        while bit < size:
            weight_rows = gather_step(weight_rows, "dom", bit)
            bit *= 2
        entry = pl.pallas_call(
            general_kernel, out_shape=shape_of(weight_rows.shape, jnp.int32), in_specs=[SMEM, VMEM], out_specs=VMEM,
        )(offset_draw, weight_rows) % total
        mine = lax.dynamic_slice_in_dim(entry[:, 0], lax.axis_index("dom") * count, count)
        padded_slots = jnp.arange(total, dtype=jnp.int32)[:, None]
        entry = jnp.broadcast_to(padded_slots + total, entry.shape)
        taken = jnp.take(lax.all_gather(padded, "dom", axis=0, tiled=True), mine, axis=0)
        padded = taken
        heavy, lights = taken[0], [taken[k] for k in range(count)]
    out, misfit = move(fields, rows, entry, obs, padded, heavy, lights)
    out = flushed(out)
    misfit = jnp.sum(summed(misfit, "space"), axis=1)
    return out.reshape(shape), -0.5 * misfit / (obs_cells.shape[0] * slabs)


def solution(mesh):
    return jax.shard_map(
        local,
        mesh=mesh,
        in_specs=(P("dom", None, "space", None), P("dom"), P(), P("space"), P("space"), P("space")),
        out_specs=(P("dom", None, "space", None), P("dom")),
        check_vma=False,
    )
```
